32 devices in a mesh: seq: 8 (over z, y), head: 4 (over x, core).
Axes of the slice: x: 2, y: 2, z: 4, core: 2. Of those that a mesh axis runs over, the one named last changes fastest.
Arguments:
- tokens: bfloat16 [24576, 768], P('seq'), may hold values from -6 to 6
- w_query: bfloat16 [768, 768], P(None, 'head'), may hold values from -0.21875 to 0.21875
- w_key: bfloat16 [768, 768], P(None, 'head'), may hold values from -0.21875 to 0.21875
- w_value: bfloat16 [768, 768], P(None, 'head'), may hold values from -0.21875 to 0.21875
- freq: float32 [64, 128], replicated, may hold values from -1.5 to 1.5
- w_out: bfloat16 [768, 768], replicated, may hold values from -0.21875 to 0.21875
- router: bfloat16 [768, 32], replicated, may hold values from -0.21875 to 0.21875
- w_in: bfloat16 [32, 768, 3072], P(('seq', 'head')), may hold values from -0.21875 to 0.21875
- w_down: bfloat16 [32, 3072, 768], P(('seq', 'head')), may hold values from -0.109375 to 0.109375
- picks: int32 [32, 32, 6], P(None, ('seq', 'head')), may hold values from 0 to 767, as said below
Outputs:
- layer_out: bfloat16 [24576, 768], P(('seq', 'head'))
The draws below stay inside these ranges and needn't reach their ends.
Inputs may be any that keep to these rules, and one draw needn't show every extreme that they name: `picks`: for each expert and each source block the 6 picked rows are distinct.
All inputs are finite; a program needn't handle non-finite values.
Results may differ from the reference program's by a relative error of at most 0.017.
Values may be sent and summed in bfloat16 or wider, within the bound.
No kernel may reach another device: no remote copies, remote signals or barrier semaphores. Data moves between devices by JAX's collectives and lax.ppermute only.
A program may use at most 128 MiB of HBM per device.

```python
import math
import jax
import jax.numpy as jnp
from jax import lax

D = 768
HEADS = 12
HD = 64
FEAT = 256
FF = 3072
BLOCK = 512
CAP = 6
TOKENS = 24576
EXPERTS = 32
ROWS = 768


def draw_picks(key, part):
    scores = jax.random.randint(key, (EXPERTS, EXPERTS, ROWS), 0, 4096)
    row_ids = jnp.arange(ROWS, dtype=jnp.int32)[None, None, :]
    expert_ids = jnp.arange(EXPERTS, dtype=jnp.int32)[:, None, None]
    first = (expert_ids == 0) & (row_ids == 0)
    last = (expert_ids == 0) & (row_ids == ROWS - 1)
    scores = jnp.where(first, -2, jnp.where(last, -1, scores))
    order = jnp.argsort(scores * ROWS + row_ids, axis=-1, stable=True)
    return order[..., :CAP].astype(jnp.int32)


def block_levels(rng, dims, pieces, smallest, top_value):
    def one(axis_at, blocks):
        steps = jax.random.uniform(jax.random.fold_in(jax.random.fold_in(rng, 6), axis_at), (blocks,), jnp.float32, smallest / len(pieces), top_value / len(pieces))
        return jnp.repeat(jnp.exp(steps), dims[axis_at] // blocks).reshape((-1,) + (1,) * (len(dims) - axis_at - 1))

    factor_of = one(*pieces[0])
    for cut in pieces[1:]:
        factor_of = factor_of * one(*cut)
    return factor_of


def bell_draw(key, extent, deviation, most, cuts=(), kind=jnp.bfloat16):
    array = jax.random.normal(key, extent, jnp.float32) * deviation
    if len(cuts) > 0:
        array = block_levels(key, extent, cuts, -0.22, 0.18) * array
    return jnp.clip(array, min=-most, max=most).astype(kind)


def setup_inputs(seed: int = 0) -> dict:
    key_of = jax.random.split(jax.random.key(seed), 11)
    tokens = bell_draw(key_of[0], (TOKENS, D), 1.0, 6.0, ((0, 8),))
    w_query = bell_draw(key_of[1], (D, D), D ** -0.5, 0.21875, ((1, 4),))
    w_key = bell_draw(key_of[2], (D, D), D ** -0.5, 0.21875, ((1, 4),))
    w_value = bell_draw(key_of[3], (D, D), D ** -0.5, 0.21875, ((1, 4),))
    freq = bell_draw(key_of[4], (HD, FEAT // 2), 0.25, 1.5, (), jnp.float32)
    w_out = bell_draw(key_of[5], (D, D), D ** -0.5, 0.21875)
    router = bell_draw(key_of[6], (D, EXPERTS), D ** -0.5, 0.21875)
    w_in = bell_draw(key_of[7], (EXPERTS, D, FF), D ** -0.5, 0.21875, ((0, 32),))
    w_down = bell_draw(key_of[8], (EXPERTS, FF, D), FF ** -0.5, 0.109375, ((0, 32),))
    picks = draw_picks(jax.random.fold_in(key_of[10], 71), 0)
    return dict(tokens=tokens, w_query=w_query, w_key=w_key, w_value=w_value, freq=freq, w_out=w_out, router=router, w_in=w_in, w_down=w_down, picks=picks)


EPS = 1e-06

def features(projected, freq, heads):
    rows = projected.shape[0]
    split = projected.reshape(rows, heads, -1).astype(jnp.float32)
    phase = jnp.einsum('thd,df->thf', split, freq, precision=lax.Precision.HIGHEST)
    scale = 1.0 / math.sqrt(freq.shape[1])
    return (jnp.concatenate([jnp.cos(phase), jnp.sin(phase)], axis=-1) * scale).astype(jnp.bfloat16)

def local_pass(qf, kf, vals, block, start_state):
    total, heads, feat = qf.shape
    width = vals.shape[2]
    count = total // block
    q_blocks = qf.reshape(count, block, heads, feat)
    k_blocks = kf.reshape(count, block, heads, feat)
    v_blocks = vals.reshape(count, block, heads, width)
    causal = jnp.arange(block)[:, None] >= jnp.arange(block)[None, :]

    def advance(state, blocks):
        q_part, k_part, v_part = blocks
        scores = jnp.einsum('bhf,chf->hbc', q_part.astype(jnp.float32), k_part.astype(jnp.float32))
        scores = jnp.where(causal[None], scores, 0.0).astype(jnp.bfloat16)
        inner = jnp.einsum('hbc,chd->bhd', scores.astype(jnp.float32), v_part.astype(jnp.float32))
        carried = jnp.einsum('bhf,hfd->bhd', q_part.astype(jnp.float32), state, precision=lax.Precision.HIGHEST)
        state = state + jnp.einsum('chf,chd->hfd', k_part.astype(jnp.float32), v_part.astype(jnp.float32))
        return (state, inner + carried)
    final, outs = lax.scan(advance, start_state, (q_blocks, k_blocks, v_blocks))
    return outs.reshape(total, heads, width)

def reference(tokens, w_query, w_key, w_value, freq, w_out, router, w_in, w_down, picks):
    query = jnp.dot(tokens, w_query, preferred_element_type=jnp.float32).astype(jnp.bfloat16)
    key = jnp.dot(tokens, w_key, preferred_element_type=jnp.float32).astype(jnp.bfloat16)
    value = jnp.dot(tokens, w_value, preferred_element_type=jnp.float32).astype(jnp.bfloat16)
    q_feat = features(query, freq, HEADS)
    k_feat = features(key, freq, HEADS)
    vals = value.reshape(TOKENS, HEADS, HD)
    start_state = jnp.zeros((HEADS, FEAT, HD), jnp.float32)
    raw = local_pass(q_feat, k_feat, vals, BLOCK, start_state)
    meansq = lax.optimization_barrier(jnp.mean(raw * raw, axis=-1, keepdims=True))
    attn = (raw * lax.rsqrt(meansq + EPS)).astype(jnp.bfloat16).reshape(TOKENS, D)
    hidden_state = (tokens.astype(jnp.float32) + jnp.dot(attn, w_out, preferred_element_type=jnp.float32)).astype(jnp.bfloat16)
    gate = jax.nn.sigmoid(jnp.dot(hidden_state, router, preferred_element_type=jnp.float32)).astype(jnp.bfloat16)
    block_rows = TOKENS // EXPERTS
    places = (jnp.arange(EXPERTS, dtype=jnp.int32)[None, :, None] * block_rows + picks).astype(jnp.int32)
    flat = places.reshape(EXPERTS, -1)

    def expert(inputs):
        place, first, second = inputs
        chosen = hidden_state[place]
        inner = jax.nn.gelu(jnp.dot(chosen, first, preferred_element_type=jnp.float32), approximate=True).astype(jnp.bfloat16)
        return jnp.dot(inner, second, preferred_element_type=jnp.float32).astype(jnp.bfloat16)
    expert_out = lax.map(expert, (flat, w_in, w_down))
    weight = gate[flat, jnp.arange(EXPERTS, dtype=jnp.int32)[:, None]]
    contrib = weight.astype(jnp.float32)[..., None] * expert_out.astype(jnp.float32)
    moe = jnp.zeros((TOKENS, D), jnp.float32).at[flat.reshape(-1)].add(contrib.reshape(-1, D))
    return (hidden_state.astype(jnp.float32) + moe).astype(jnp.bfloat16)
```

```python
import functools
import math

import jax
import jax.numpy as jnp
from jax import lax
from jax.experimental import pallas as pl
from jax.experimental.pallas import tpu as pltpu
from jax.sharding import PartitionSpec as P

HD = 64
EPS = 1e-06
CHUNK = 256
PAD = 8
BF = jnp.bfloat16
F32 = jnp.float32
MIB = 2**20
SIN = (3.14158202, -5.16714279, 2.54189901, -0.55463616)
COS = (0.9999933, -4.93393802, 4.04128381, -1.22212701)


def nn(a, b):
    return lax.dot_general(a, b, (((1,), (0,)), ((), ())), preferred_element_type=F32)


def nt(a, b):
    return lax.dot_general(a, b, (((1,), (1,)), ((), ())), preferred_element_type=F32)


def tn(a, b):
    return lax.dot_general(a, b, (((0,), (0,)), ((), ())), preferred_element_type=F32)


def wave(turns, scale):
    big = F32(1.5 * 2.0**23)
    r = turns - ((turns + big) - big)
    u = r * r
    root = math.sqrt(2 * scale)
    a = [F32(v * root) for v in SIN]
    b = [F32(v * root) for v in COS]
    s = r * (a[0] + u * (a[1] + u * (a[2] + u * a[3])))
    c = b[0] + u * (b[1] + u * (b[2] + u * b[3]))
    return F32(scale) - s * s, s * c


def parts(f):
    hi = f.astype(BF)
    rest = f - hi.astype(F32)
    mid = rest.astype(BF)
    lo = (rest - mid.astype(F32)).astype(BF)
    return [hi, mid, lo]


def whole(shape):
    return pl.BlockSpec(shape, lambda *_: (0,) * len(shape))


def params(mib=40):
    return pltpu.CompilerParams(vmem_limit_bytes=mib * MIB)


def cost(flops, nbytes):
    return pl.CostEstimate(flops=int(flops), bytes_accessed=int(nbytes), transcendentals=0)


def key_kernel(tok_ref, wk_ref, wvt_ref, freq_ref, kf_ref, vt_ref, sc_ref, tot_ref, f3, st):
    heads = wk_ref.shape[1] // HD
    half = freq_ref.shape[1]

    @pl.when(pl.program_id(0) == 0)
    def _():
        f3[...] = jnp.concatenate(parts(freq_ref[...] * F32(0.5 / math.pi)), axis=0)
        st[...] = jnp.zeros_like(st)

    tok = tok_ref[...]
    k = nn(tok, wk_ref[...]).astype(BF)
    vt = nt(wvt_ref[...], tok).astype(BF)
    vt_ref[...] = vt
    for h in range(heads):
        kh = k[:, h * HD : (h + 1) * HD]
        phase = nn(jnp.concatenate([kh] * 3, axis=1), f3[...])
        c, s = wave(phase, 1 / math.sqrt(half))
        kf = jnp.concatenate([c.astype(BF), s.astype(BF)], axis=1)
        kf_ref[:, h * 2 * half : (h + 1) * 2 * half] = kf
        mine = slice(h * HD, (h + 1) * HD)
        acc = st[mine, :]
        for j in range(tok.shape[0] // CHUNK):
            sc_ref[j, mine, :] = acc.astype(BF)
            rows = slice(j * CHUNK, (j + 1) * CHUNK)
            acc = acc + nn(vt[mine, rows], kf[rows])
        st[mine, :] = acc
    tot_ref[...] = st[...].astype(BF)


def key_pass(tokens, w_key, wvt, freq, rows):
    total, d = tokens.shape
    wid = w_key.shape[1]
    feat = 2 * freq.shape[1]
    heads = wid // HD
    return pl.pallas_call(
        key_kernel,
        grid=(total // rows,),
        in_specs=[
            pl.BlockSpec((rows, d), lambda i: (i, 0)),
            whole(w_key.shape),
            whole(wvt.shape),
            whole(freq.shape),
        ],
        out_specs=[
            pl.BlockSpec((rows, heads * feat), lambda i: (i, 0)),
            pl.BlockSpec((wid, rows), lambda i: (0, i)),
            pl.BlockSpec((rows // CHUNK, wid, feat), lambda i: (i, 0, 0)),
            whole((wid, feat)),
        ],
        out_shape=[
            jax.ShapeDtypeStruct((total, heads * feat), BF),
            jax.ShapeDtypeStruct((wid, total), BF),
            jax.ShapeDtypeStruct((total // CHUNK, wid, feat), BF),
            jax.ShapeDtypeStruct((wid, feat), BF),
        ],
        scratch_shapes=[pltpu.VMEM((3 * HD, freq.shape[1]), BF), pltpu.VMEM((wid, feat), F32)],
        compiler_params=params(),
        cost_estimate=cost(5e9, 12e6),
        name="key_pass",
    )(tokens, w_key, wvt, freq)


def query_kernel(tok_ref, wqt_ref, ft_ref, kf_ref, vt_ref, sc_ref, *rest):
    qft_ref, raw_ref, f3t = rest[-3:]
    heads = wqt_ref.shape[0] // HD
    half = ft_ref.shape[0]
    feat = 2 * half

    @pl.when(pl.program_id(0) == 0)
    def _():
        f3t[...] = jnp.concatenate(parts(ft_ref[...] * F32(0.5 / math.pi)), axis=1)

    tok = tok_ref[...]
    qt = nt(wqt_ref[...], tok).astype(BF)
    place = [lax.broadcasted_iota(jnp.int32, (CHUNK, CHUNK), i) for i in (0, 1)]
    keep = place[0] <= place[1]
    for h in range(heads):
        mine = slice(h * HD, (h + 1) * HD)
        phase = nn(f3t[...], jnp.concatenate([qt[mine]] * 3, axis=0))
        c, s = wave(phase, 1 / math.sqrt(half))
        qf = jnp.concatenate([c.astype(BF), s.astype(BF)], axis=0)
        qft_ref[h * feat : (h + 1) * feat, :] = qf
        for j in range(tok.shape[0] // CHUNK):
            cols = slice(j * CHUNK, (j + 1) * CHUNK)
            both = jnp.concatenate([kf_ref[cols, h * feat : (h + 1) * feat], sc_ref[j, mine, :]], axis=0)
            both = nn(both, qf[:, cols])
            scores = jnp.where(keep, both[:CHUNK], 0.0).astype(BF)
            raw_ref[mine, cols] = nn(vt_ref[mine, cols], scores) + both[CHUNK:]


def query_pass(tokens, wqt, freq_t, kf, vt, sc, rows, first, count, into=None):
    total, d = tokens.shape
    wid = wqt.shape[0]
    feat = 2 * freq_t.shape[0]
    heads = wid // HD
    held = [] if into is None else list(into)
    return pl.pallas_call(
        query_kernel,
        grid=(count,),
        in_specs=[
            pl.BlockSpec((rows, d), lambda i: (i + first, 0)),
            whole(wqt.shape),
            whole(freq_t.shape),
            pl.BlockSpec((rows, heads * feat), lambda i: (i + first, 0)),
            pl.BlockSpec((wid, rows), lambda i: (0, i + first)),
            pl.BlockSpec((rows // CHUNK, wid, feat), lambda i: (i + first, 0, 0)),
        ]
        + [pl.BlockSpec(memory_space=pl.ANY)] * len(held),
        out_specs=[
            pl.BlockSpec((heads * feat, rows), lambda i: (0, i + first)),
            pl.BlockSpec((wid, rows), lambda i: (0, i + first)),
        ],
        out_shape=[
            jax.ShapeDtypeStruct((heads * feat, total), BF),
            jax.ShapeDtypeStruct((wid, total), F32),
        ],
        input_output_aliases={6 + i: i for i in range(len(held))},
        scratch_shapes=[pltpu.VMEM((freq_t.shape[0], 3 * HD), BF)],
        compiler_params=params(),
        cost_estimate=cost(1.5e9 * count, 4e6 * count),
        name="query_pass",
    )(tokens, wqt, freq_t, kf, vt, sc, *held)


def prefix_states(mine):
    size = lax.axis_size("seq")
    at = lax.axis_index("seq")
    held = mine
    before = jnp.zeros(mine.shape, F32)
    stride = 1
    while stride < size:
        radix = 2 if (size // stride).bit_length() % 2 == 0 else 4
        last = stride * radix >= size
        total = held.astype(F32)
        for k in range(1, radix):
            step = k * stride
            pairs = [(i, i ^ step) for i in range(size) if not last or i < i ^ step]
            value = lax.ppermute(held, "seq", pairs).astype(F32)
            total = total + value
            before = before + jnp.where((at ^ step) < at, value, 0.0)
        held = total.astype(BF)
        stride *= radix
    return before.astype(BF)


def norm_kernel(slots, me_ref, raw_ref, qft_ref, pre_ref, pick_ref, *rest):
    outs, sent_ref, acc = rest[:slots], rest[slots], rest[slots + 1]
    step = pl.program_id(0)
    heads = raw_ref.shape[0] // HD
    feat = pre_ref.shape[1]
    rows = raw_ref.shape[1]
    normed = []
    for h in range(heads):
        mine = slice(h * HD, (h + 1) * HD)
        raw = raw_ref[mine, :] + nn(pre_ref[mine, :], qft_ref[h * feat : (h + 1) * feat, :])
        meansq = jnp.mean(raw * raw, axis=0, keepdims=True)
        normed.append((raw * lax.rsqrt(meansq + F32(EPS))).astype(BF))
    attn = jnp.concatenate(normed, axis=0)
    for k in range(slots):

        @pl.when(step == k)
        def _():
            outs[k][...] = attn

    at = lax.broadcasted_iota(jnp.int32, (pick_ref.shape[0], rows), 1) + (me_ref[0] ^ step) * rows
    onehot = (pick_ref[...] == at).astype(F32).astype(BF)
    picked = nt(onehot, attn)

    @pl.when(step == 0)
    def _():
        acc[...] = picked

    @pl.when(step > 0)
    def _():
        acc[...] += picked

    @pl.when(step == slots - 1)
    def _():
        sent_ref[...] = acc[...].astype(BF)


def norm_pass(me, raw, qft, pre, pick_col, slots):
    wid, total = raw.shape
    rows = total // slots
    n = pick_col.shape[0]
    block = lambda i, me_ref: (0, me_ref[0] ^ i)
    return pl.pallas_call(
        functools.partial(norm_kernel, slots),
        grid_spec=pltpu.PrefetchScalarGridSpec(
            num_scalar_prefetch=1,
            grid=(slots,),
            in_specs=[
                pl.BlockSpec((wid, rows), block),
                pl.BlockSpec((qft.shape[0], rows), block),
                whole(pre.shape),
                whole(pick_col.shape),
            ],
            out_specs=[whole((wid, rows))] * slots + [whole((n, wid))],
            scratch_shapes=[pltpu.VMEM((n, wid), F32)],
        ),
        out_shape=[jax.ShapeDtypeStruct((wid, rows), BF)] * slots + [jax.ShapeDtypeStruct((n, wid), BF)],
        compiler_params=params(),
        cost_estimate=cost(3e9, 8e6),
        name="norm_pass",
    )(me, raw, qft, pre, pick_col)


def select_kernel(tok_ref, pick_ref, out_ref, acc):
    step = pl.program_id(0)
    rows = tok_ref.shape[0]
    at = lax.broadcasted_iota(jnp.int32, (pick_ref.shape[0], rows), 1) + step * rows
    onehot = (pick_ref[...] == at).astype(F32).astype(BF)
    picked = nn(onehot, tok_ref[...])

    @pl.when(step == 0)
    def _():
        acc[...] = picked

    @pl.when(step > 0)
    def _():
        acc[...] += picked

    out_ref[...] = acc[...].astype(BF)


def select_rows(tokens, pick_col, rows):
    total, d = tokens.shape
    n = pick_col.shape[0]
    return pl.pallas_call(
        select_kernel,
        grid=(total // rows,),
        in_specs=[pl.BlockSpec((rows, d), lambda i: (i, 0)), whole(pick_col.shape)],
        out_specs=whole((n, d)),
        out_shape=jax.ShapeDtypeStruct((n, d), BF),
        scratch_shapes=[pltpu.VMEM((n, d), F32)],
        compiler_params=params(),
        cost_estimate=cost(1e9, 5e6),
        name="select_rows",
    )(tokens, pick_col)


def expert_kernel(cap, attn_ref, tok_ref, wo_ref, wi_ref, wd_ref, out_ref, taken, acc):
    step = pl.program_id(0)
    n, d = tok_ref.shape

    @pl.when(step == 0)
    def _():
        mixed = tok_ref[...].astype(F32)
        for h in range(wo_ref.shape[0]):
            part = attn_ref[:, h]
            mixed = mixed + nn(part.reshape(n, part.shape[-1]), wo_ref[h])
        taken[...] = mixed.astype(BF)
        acc[...] = jnp.zeros_like(acc)

    inner = jax.nn.gelu(nn(taken[...], wi_ref[0]), approximate=True).astype(BF)
    acc[...] += nn(inner, wd_ref[0])

    @pl.when(step == pl.num_programs(0) - 1)
    def _():
        m = out_ref.shape[0]
        slot = lax.broadcasted_iota(jnp.int32, (m, n), 0)
        row = lax.broadcasted_iota(jnp.int32, (m, n), 1)
        spread = ((slot // PAD) * cap + slot % PAD == row) & (slot % PAD < cap)
        out_ref[...] = nn(spread.astype(F32).astype(BF), acc[...].astype(BF)).astype(BF)


def expert_pass(arrived, tok_sel, w_out, w_in, w_down, cap, tiles=6):
    n, d = tok_sel.shape
    ff = w_in.shape[2]
    m = n // cap * PAD
    return pl.pallas_call(
        functools.partial(expert_kernel, cap),
        grid=(tiles,),
        in_specs=[
            whole(arrived.shape),
            whole(tok_sel.shape),
            whole(w_out.shape),
            pl.BlockSpec((1, d, ff // tiles), lambda i: (0, 0, i)),
            pl.BlockSpec((1, ff // tiles, d), lambda i: (0, i, 0)),
        ],
        out_specs=whole((m, d)),
        out_shape=jax.ShapeDtypeStruct((m, d), BF),
        scratch_shapes=[pltpu.VMEM((n, d), BF), pltpu.VMEM((n, d), F32)],
        compiler_params=params(),
        cost_estimate=cost(2e9, 12e6),
        name="expert_pass",
    )(arrived, tok_sel, w_out, w_in, w_down)


def hidden_kernel(slots, me_ref, tok_ref, wo_ref, router_ref, pick_ref, *rest):
    attns, hid_ref, comb_ref = rest[:slots], rest[slots], rest[slots + 1]
    mixed = tok_ref[...].astype(F32)
    for k in range(slots):
        mixed = mixed + tn(attns[k][...], wo_ref[me_ref[0] ^ k])
    hidden = mixed.astype(BF)
    hid_ref[...] = hidden
    gate = jax.nn.sigmoid(nn(hidden, router_ref[...])).astype(BF)
    e, n = gate.shape[1], pick_ref.shape[1]
    source = lax.broadcasted_iota(jnp.int32, (e, n), 0)
    slot = lax.broadcasted_iota(jnp.int32, (e, n), 1)
    spread = nn(gate, (slot // PAD == source).astype(F32).astype(BF))
    at = lax.broadcasted_iota(jnp.int32, (hidden.shape[0], n), 0)
    comb_ref[...] = jnp.where(pick_ref[...] == at, spread, 0.0).astype(BF)


def hidden_pass(me, tokens, w_out, router, pick_row, attns, rows):
    d = tokens.shape[1]
    slots = len(attns)
    n = pick_row.shape[1]
    return pl.pallas_call(
        functools.partial(hidden_kernel, slots),
        grid_spec=pltpu.PrefetchScalarGridSpec(
            num_scalar_prefetch=1,
            grid=(1,),
            in_specs=[
                pl.BlockSpec((rows, d), lambda i, me_ref: (me_ref[0], 0)),
                whole(w_out.shape),
                whole(router.shape),
                whole(pick_row.shape),
            ]
            + [whole(a.shape) for a in attns],
            out_specs=[whole((rows, d)), whole((rows, n))],
        ),
        out_shape=[jax.ShapeDtypeStruct((rows, d), BF), jax.ShapeDtypeStruct((rows, n), BF)],
        compiler_params=params(),
        cost_estimate=cost(2e9, 6e6),
        name="hidden_pass",
    )(me, tokens, w_out, router, pick_row, *attns)


def combine_kernel(hid_ref, comb_ref, back_ref, out_ref):
    out_ref[...] = (hid_ref[...].astype(F32) + nn(comb_ref[...], back_ref[...])).astype(BF)


def combine_pass(hidden, comb, back):
    rows, d = hidden.shape
    n = comb.shape[1]
    tiles = 2
    return pl.pallas_call(
        combine_kernel,
        grid=(tiles,),
        in_specs=[
            pl.BlockSpec((rows // tiles, d), lambda i: (i, 0)),
            pl.BlockSpec((rows // tiles, n), lambda i: (i, 0)),
            whole(back.shape),
        ],
        out_specs=pl.BlockSpec((rows // tiles, d), lambda i: (i, 0)),
        out_shape=jax.ShapeDtypeStruct((rows, d), BF),
        compiler_params=params(),
        cost_estimate=cost(5e8, 4e6),
        name="combine_pass",
    )(hidden, comb, back)


def per_device(tokens, w_query, w_key, w_value, freq, w_out, router, w_in, w_down, picks):
    total, d = tokens.shape
    group = lax.axis_size("head")
    ring = lax.axis_size("seq")
    me = lax.axis_index("head")
    me_arr = me.astype(jnp.int32)[None]
    rows = total // group
    experts, _, cap = picks.shape
    wid = w_query.shape[1]

    own = picks[:, 0, :]
    near = [own]
    for k in range(1, group):
        near.append(lax.ppermute(own, "head", [(i, i ^ k) for i in range(group)]))
    block = jnp.arange(group, dtype=jnp.int32)
    slot = block ^ me
    ordered = sum(
        jnp.where((slot == k)[None, :, None], near[k][:, None, :], 0) for k in range(group)
    )
    ordered = ordered + block[None, :, None] * rows
    pick_col = ordered.reshape(experts * group * cap, 1)
    mine_col = lax.dynamic_index_in_dim(
        ordered.reshape(ring, group, group * cap), me, axis=1, keepdims=False
    ).reshape(ring * group * cap, 1)
    pick_row = jnp.pad(own, ((0, 0), (0, PAD - cap)), constant_values=-1).reshape(1, experts * PAD)

    chosen = select_rows(tokens, mine_col, rows).reshape(ring, group * cap, d)
    tok_sel = lax.all_to_all(chosen, "seq", split_axis=0, concat_axis=0, tiled=True)
    tok_sel = tok_sel.reshape(ring * group * cap, d)

    kf, vt, sc, state = key_pass(tokens, w_key, w_value.T, freq, rows)
    pre = prefix_states(state)
    wqt, freq_t = w_query.T, freq.T
    held = query_pass(tokens, wqt, freq_t, kf, vt, sc, rows, 0, 1)
    qft, raw = query_pass(tokens, wqt, freq_t, kf, vt, sc, rows, 1, group - 1, held)
    *attns, sent = norm_pass(me_arr, raw, qft, pre, pick_col, group)

    sent = sent.reshape(experts, group * cap, wid)
    arrived = lax.all_to_all(sent, ("seq", "head"), split_axis=0, concat_axis=0, tiled=True)
    attns = [attns[0]] + [
        lax.ppermute(attns[k], "head", [(i, i ^ k) for i in range(group)]) for k in range(1, group)
    ]
    w_out = w_out.reshape(group, wid, d)
    result = expert_pass(
        arrived.reshape(ring, group, group * cap, wid), tok_sel, w_out, w_in, w_down, cap
    )
    back = lax.all_to_all(
        result.reshape(experts, PAD, d), ("seq", "head"), split_axis=0, concat_axis=0, tiled=True
    )
    hidden, comb = hidden_pass(me_arr, tokens, w_out, router, pick_row, attns, rows)
    return combine_pass(hidden, comb, back.reshape(experts * PAD, d))


def solution(mesh):
    in_specs = (
        P("seq", None),
        P(None, "head"),
        P(None, "head"),
        P(None, "head"),
        P(),
        P(),
        P(),
        P(("seq", "head"), None, None),
        P(("seq", "head"), None, None),
        P(None, ("seq", "head"), None),
    )
    out_specs = P(("seq", "head"), None)
    return jax.shard_map(
        per_device, mesh=mesh, in_specs=in_specs, out_specs=out_specs, check_vma=False
    )
```

```python
import functools
import math

import jax
import jax.numpy as jnp
from jax import lax
from jax.experimental import pallas as pl
from jax.experimental.pallas import tpu as pltpu
from jax.sharding import PartitionSpec as P

HD = 64
EPS = 1e-06
CHUNK = 256
PAD = 8
BF = jnp.bfloat16
F32 = jnp.float32
MIB = 2**20
SIN = (3.14158202, -5.16714279, 2.54189901, -0.55463616)
COS = (0.9999933, -4.93393802, 4.04128381, -1.22212701)


def nn(a, b):
    return lax.dot_general(a, b, (((1,), (0,)), ((), ())), preferred_element_type=F32)


def nt(a, b):
    return lax.dot_general(a, b, (((1,), (1,)), ((), ())), preferred_element_type=F32)


def tn(a, b):
    return lax.dot_general(a, b, (((0,), (0,)), ((), ())), preferred_element_type=F32)


def wave(turns, scale):
    big = F32(1.5 * 2.0**23)
    r = turns - ((turns + big) - big)
    u = r * r
    root = math.sqrt(2 * scale)
    a = [F32(v * root) for v in SIN]
    b = [F32(v * root) for v in COS]
    s = r * (a[0] + u * (a[1] + u * (a[2] + u * a[3])))
    c = b[0] + u * (b[1] + u * (b[2] + u * b[3]))
    return F32(scale) - s * s, s * c


def parts(f):
    hi = f.astype(BF)
    rest = f - hi.astype(F32)
    mid = rest.astype(BF)
    lo = (rest - mid.astype(F32)).astype(BF)
    return [hi, mid, lo]


def whole(shape):
    return pl.BlockSpec(shape, lambda *_: (0,) * len(shape))


def params(mib=60):
    return pltpu.CompilerParams(vmem_limit_bytes=mib * MIB)


def cost(flops, nbytes):
    return pl.CostEstimate(flops=int(flops), bytes_accessed=int(nbytes), transcendentals=0)


def key_kernel(tok_ref, wkt_ref, wvt_ref, freq_ref, kf_ref, vt_ref, sc_ref, tot_ref, f3, st):
    heads = wkt_ref.shape[0] // HD
    half = freq_ref.shape[1]

    @pl.when(pl.program_id(0) == 0)
    def _():
        f3[...] = jnp.concatenate(parts(freq_ref[...] * F32(0.5 / math.pi)), axis=0)
        st[...] = jnp.zeros_like(st)

    tok = tok_ref[...]
    k = nt(tok, wkt_ref[...]).astype(BF)
    vt = nt(wvt_ref[...], tok).astype(BF)
    vt_ref[...] = vt
    for h in range(heads):
        kh = k[:, h * HD : (h + 1) * HD]
        phase = nn(jnp.concatenate([kh] * 3, axis=1), f3[...])
        c, s = wave(phase, 1 / math.sqrt(half))
        kf = jnp.concatenate([c.astype(BF), s.astype(BF)], axis=1)
        kf_ref[:, h * 2 * half : (h + 1) * 2 * half] = kf
        mine = slice(h * HD, (h + 1) * HD)
        acc = st[mine, :]
        for j in range(tok.shape[0] // CHUNK):
            sc_ref[j, mine, :] = acc.astype(BF)
            rows = slice(j * CHUNK, (j + 1) * CHUNK)
            acc = acc + nn(vt[mine, rows], kf[rows])
        st[mine, :] = acc

    @pl.when(pl.program_id(0) == pl.num_programs(0) - 1)
    def _():
        state = st[...].astype(BF)
        for i in range(tot_ref.shape[0]):
            tot_ref[i] = state


def key_pass(tokens, wkt, wvt, freq, rows, copies):
    total, d = tokens.shape
    wid = wkt.shape[0]
    feat = 2 * freq.shape[1]
    heads = wid // HD
    return pl.pallas_call(
        key_kernel,
        grid=(total // rows,),
        in_specs=[
            pl.BlockSpec((rows, d), lambda i: (i, 0)),
            whole(wkt.shape),
            whole(wvt.shape),
            whole(freq.shape),
        ],
        out_specs=[
            pl.BlockSpec((rows, heads * feat), lambda i: (i, 0)),
            pl.BlockSpec((wid, rows), lambda i: (0, i)),
            pl.BlockSpec((rows // CHUNK, wid, feat), lambda i: (i, 0, 0)),
            whole((copies, wid, feat)),
        ],
        out_shape=[
            jax.ShapeDtypeStruct((total, heads * feat), BF),
            jax.ShapeDtypeStruct((wid, total), BF),
            jax.ShapeDtypeStruct((total // CHUNK, wid, feat), BF),
            jax.ShapeDtypeStruct((copies, wid, feat), BF),
        ],
        scratch_shapes=[pltpu.VMEM((3 * HD, freq.shape[1]), BF), pltpu.VMEM((wid, feat), F32)],
        compiler_params=params(),
        cost_estimate=cost(5e9, 12e6),
        name="key_pass",
    )(tokens, wkt, wvt, freq)


def chosen(slot, pick_refs):
    row = pick_refs[0][...]
    for k in range(1, len(pick_refs)):
        row = jnp.where(slot == k, pick_refs[k][...], row)
    return row


def marks(row, rows):
    at = lax.broadcasted_iota(jnp.int32, (rows, row.shape[1]), 0)
    return (at == row).astype(F32).astype(BF)


def query_kernel(slots, me_ref, tok_ref, wqt_ref, ft_ref, kf_ref, vt_ref, sc_ref, *rest):
    pick_refs = rest[:slots]
    qft_ref, raw_ref, seen_ref, f3t, both_w = rest[slots:]
    wid, d = wqt_ref.shape
    heads = wid // HD
    half = ft_ref.shape[0]
    feat = 2 * half
    step = pl.program_id(0)

    @pl.when(step == 0)
    def _():
        f3t[...] = jnp.concatenate(parts(ft_ref[...] * F32(0.5 / math.pi)), axis=1)
        both_w[:wid] = wqt_ref[...]
        line = lax.broadcasted_iota(jnp.int32, (wid, d), 0)
        column = lax.broadcasted_iota(jnp.int32, (wid, d), 1)
        both_w[wid:] = (line + me_ref[0] * wid == column).astype(F32).astype(BF)

    tok = tok_ref[...]
    out = nt(both_w[...], tok).astype(BF)
    qt = out[:wid]
    seen_ref[0] = nn(out[wid:], marks(chosen(me_ref[0] ^ step, pick_refs), tok.shape[0])).astype(BF)
    place = [lax.broadcasted_iota(jnp.int32, (CHUNK, CHUNK), i) for i in (0, 1)]
    keep = place[0] <= place[1]
    for h in range(heads):
        mine = slice(h * HD, (h + 1) * HD)
        phase = nn(f3t[...], jnp.concatenate([qt[mine]] * 3, axis=0))
        c, s = wave(phase, 1 / math.sqrt(half))
        qf = jnp.concatenate([c.astype(BF), s.astype(BF)], axis=0)
        qft_ref[h * feat : (h + 1) * feat, :] = qf
        for j in range(tok.shape[0] // CHUNK):
            cols = slice(j * CHUNK, (j + 1) * CHUNK)
            both = jnp.concatenate([kf_ref[cols, h * feat : (h + 1) * feat], sc_ref[j, mine, :]], axis=0)
            both = nn(both, qf[:, cols])
            scores = jnp.where(keep, both[:CHUNK], 0.0).astype(BF)
            raw_ref[mine, cols] = nn(vt_ref[mine, cols], scores) + both[CHUNK:]


def query_pass(me, tokens, wqt, freq_t, kf, vt, sc, picks):
    total, d = tokens.shape
    slots = len(picks)
    rows = total // slots
    n = picks[0].shape[1]
    wid = wqt.shape[0]
    feat = 2 * freq_t.shape[0]
    heads = wid // HD
    return pl.pallas_call(
        functools.partial(query_kernel, slots),
        grid_spec=pltpu.PrefetchScalarGridSpec(
            num_scalar_prefetch=1,
            grid=(slots,),
            in_specs=[
                pl.BlockSpec((rows, d), lambda i, m: (i, 0)),
                whole(wqt.shape),
                whole(freq_t.shape),
                pl.BlockSpec((rows, heads * feat), lambda i, m: (i, 0)),
                pl.BlockSpec((wid, rows), lambda i, m: (0, i)),
                pl.BlockSpec((rows // CHUNK, wid, feat), lambda i, m: (i, 0, 0)),
            ]
            + [whole(p.shape) for p in picks],
            out_specs=[
                pl.BlockSpec((heads * feat, rows), lambda i, m: (0, i)),
                pl.BlockSpec((wid, rows), lambda i, m: (0, i)),
                pl.BlockSpec((1, wid, n), lambda i, m: (i, 0, 0)),
            ],
            scratch_shapes=[pltpu.VMEM((freq_t.shape[0], 3 * HD), BF), pltpu.VMEM((2 * wid, d), BF)],
        ),
        out_shape=[
            jax.ShapeDtypeStruct((heads * feat, total), BF),
            jax.ShapeDtypeStruct((wid, total), F32),
            jax.ShapeDtypeStruct((slots, wid, n), BF),
        ],
        compiler_params=params(),
        cost_estimate=cost(6e9, 16e6),
        name="query_pass",
    )(me, tokens, wqt, freq_t, kf, vt, sc, *picks)


def norm_kernel(slots, cap, me_ref, raw_ref, qft_ref, states_ref, seen_ref, *rest):
    pick_refs, outs = rest[:slots], rest[slots : 2 * slots]
    sent_ref, acc, pre_ref = rest[2 * slots :]
    step = pl.program_id(0)
    block = me_ref[0] ^ step
    heads = raw_ref.shape[0] // HD
    feat = pre_ref.shape[1]

    @pl.when(step == 0)
    def _():
        before = jnp.zeros(pre_ref.shape, F32)
        for i in range(states_ref.shape[0]):
            before = before + jnp.where(i < me_ref[1], states_ref[i].astype(F32), 0.0)
        pre_ref[...] = before.astype(BF)
        acc[...] = jnp.zeros_like(acc)

    normed = []
    for h in range(heads):
        mine = slice(h * HD, (h + 1) * HD)
        raw = raw_ref[mine, :] + nn(pre_ref[mine, :], qft_ref[h * feat : (h + 1) * feat, :])
        meansq = jnp.mean(raw * raw, axis=0, keepdims=True)
        normed.append((raw * lax.rsqrt(meansq + F32(EPS))).astype(BF))
    attn = jnp.concatenate(normed, axis=0)
    for k in range(slots):

        @pl.when(step == k)
        def _():
            outs[k][...] = attn

    picked = nn(attn, marks(chosen(step, pick_refs), attn.shape[1])).astype(BF)
    both = jnp.concatenate([picked, seen_ref[0]], axis=0)
    n = both.shape[1]
    experts = n // cap
    at = lax.broadcasted_iota(jnp.int32, (1, n), 1)
    row = (at % experts * slots + block) * cap + at // experts
    acc[...] += nt(marks(row, acc.shape[0]), both)

    @pl.when(step == slots - 1)
    def _():
        sent_ref[...] = acc[...].astype(BF)


def norm_pass(me, raw, qft, states, seen, picks, cap):
    wid, total = raw.shape
    slots = len(picks)
    rows = total // slots
    n = slots * picks[0].shape[1]
    block = lambda i, m: (0, m[0] ^ i)
    return pl.pallas_call(
        functools.partial(norm_kernel, slots, cap),
        grid_spec=pltpu.PrefetchScalarGridSpec(
            num_scalar_prefetch=1,
            grid=(slots,),
            in_specs=[
                pl.BlockSpec((wid, rows), block),
                pl.BlockSpec((qft.shape[0], rows), block),
                whole(states.shape),
                pl.BlockSpec((1,) + seen.shape[1:], lambda i, m: (m[0] ^ i, 0, 0)),
            ]
            + [whole(p.shape) for p in picks],
            out_specs=[whole((wid, rows))] * slots + [whole((n, 2 * wid))],
            scratch_shapes=[pltpu.VMEM((n, 2 * wid), F32), pltpu.VMEM(states.shape[1:], BF)],
        ),
        out_shape=[jax.ShapeDtypeStruct((wid, rows), BF)] * slots
        + [jax.ShapeDtypeStruct((n, 2 * wid), BF)],
        compiler_params=params(),
        cost_estimate=cost(3e9, 8e6),
        name="norm_pass",
    )(me, raw, qft, states, seen, *picks)


def expert_kernel(cap, tiles, got_hbm, wo_hbm, wi_hbm, wd_hbm, out_ref, got, wo, wi, wd, taken, acc, sems):
    slots, ring, each, both = got.shape
    wid = both // 2
    n, d = ring * each, wo.shape[2]
    ff = wi.shape[1]
    tile = ff // tiles
    landing = [pltpu.make_async_copy(got_hbm.at[:, h], got.at[h], sems.at[h]) for h in range(slots)]
    copies = [pltpu.make_async_copy(wo_hbm, wo, sems.at[slots])]
    first = slots + 1
    for t in range(tiles):
        cut = pl.ds(t * tile, tile)
        copies.append(pltpu.make_async_copy(wi_hbm.at[0, :, cut], wi.at[:, cut], sems.at[first + 2 * t]))
        copies.append(pltpu.make_async_copy(wd_hbm.at[0, cut, :], wd.at[cut, :], sems.at[first + 1 + 2 * t]))
    for c in landing + copies:
        c.start()
    for c in landing:
        c.wait()
    parts_in = [got[h].reshape(n, both) for h in range(slots)]
    mixed = jnp.concatenate([g.astype(F32)[:, wid:] for g in parts_in], axis=1)
    copies[0].wait()
    for h, g in enumerate(parts_in):
        mixed = mixed + nn(g[:, :wid], wo[h])
    taken[...] = mixed.astype(BF)
    acc[...] = jnp.zeros((n, d), F32)
    for t in range(tiles):
        cut = slice(t * tile, (t + 1) * tile)
        copies[1 + 2 * t].wait()
        inner = jax.nn.gelu(nn(taken[...], wi[:, cut]), approximate=True).astype(BF)
        copies[2 + 2 * t].wait()
        acc[...] += nn(inner, wd[cut, :])
    m = out_ref.shape[0]
    at = lax.broadcasted_iota(jnp.int32, (1, n), 1)
    out_ref[...] = nn(marks(at // cap * PAD + at % cap, m), acc[...].astype(BF)).astype(BF)


def expert_pass(arrived, w_out, w_in, w_down, cap, tiles=6):
    ring, slots, each, both = arrived.shape
    d, ff = w_in.shape[1:]
    m = ring * each // cap * PAD
    return pl.pallas_call(
        functools.partial(expert_kernel, cap, tiles),
        in_specs=[pl.BlockSpec(memory_space=pl.ANY)] * 4,
        out_specs=pl.BlockSpec(memory_space=pltpu.VMEM),
        out_shape=jax.ShapeDtypeStruct((m, d), BF),
        scratch_shapes=[
            pltpu.VMEM((slots, ring, each, both), BF),
            pltpu.VMEM(w_out.shape, BF),
            pltpu.VMEM((d, ff), BF),
            pltpu.VMEM((ff, d), BF),
            pltpu.VMEM((ring * each, d), BF),
            pltpu.VMEM((ring * each, d), F32),
            pltpu.SemaphoreType.DMA((slots + 1 + 2 * tiles,)),
        ],
        compiler_params=params(),
        cost_estimate=cost(2e9, 12e6),
        name="expert_pass",
    )(arrived, w_out, w_in, w_down)


def mix_kernel(slots, me_ref, tok_ref, wo_ref, *rest):
    attns, out_ref = rest[:-1], rest[-1]
    mixed = tok_ref[...].astype(F32)
    for k in slots:
        mixed = mixed + tn(attns[k][...], wo_ref[me_ref[0] ^ k])
    out_ref[...] = mixed


def mix_pass(me, tokens, w_out, attns, rows):
    d = tokens.shape[1]
    return pl.pallas_call(
        functools.partial(mix_kernel, range(len(attns))),
        grid_spec=pltpu.PrefetchScalarGridSpec(
            num_scalar_prefetch=1,
            grid=(1,),
            in_specs=[pl.BlockSpec((rows, d), lambda i, m: (m[0], 0)), whole(w_out.shape)]
            + [whole(a.shape) for a in attns],
            out_specs=whole((rows, d)),
        ),
        out_shape=jax.ShapeDtypeStruct((rows, d), F32),
        compiler_params=params(),
        cost_estimate=cost(2e9, 6e6),
        name="mix_pass",
    )(me, tokens, w_out, *attns)


def combine_kernel(me_ref, mix_ref, wo_ref, attn_ref, router_ref, pick_ref, back_ref, out_ref):
    hidden = (mix_ref[...] + tn(attn_ref[...], wo_ref[0])).astype(BF)
    gate = jax.nn.sigmoid(nt(hidden, router_ref[...])).astype(BF)
    e, n = gate.shape[1], pick_ref.shape[1]
    rows = hidden.shape[0]
    source = lax.broadcasted_iota(jnp.int32, (1, n), 1) // PAD
    spread = nn(gate, marks(source, e))
    at = lax.broadcasted_iota(jnp.int32, (rows, n), 0) + pl.program_id(0) * rows
    comb = jnp.where(pick_ref[...] == at, spread, 0.0).astype(BF)
    out_ref[...] = (hidden.astype(F32) + nn(comb, back_ref[...])).astype(BF)


def combine_pass(me, mixed, w_out, attn, router_t, pick_row, back, tiles=3):
    rows, d = mixed.shape
    last = w_out.shape[0] - 1
    tile = rows // tiles
    return pl.pallas_call(
        combine_kernel,
        grid_spec=pltpu.PrefetchScalarGridSpec(
            num_scalar_prefetch=1,
            grid=(tiles,),
            in_specs=[
                pl.BlockSpec((tile, d), lambda i, m: (i, 0)),
                pl.BlockSpec((1,) + w_out.shape[1:], lambda i, m: (m[0] ^ last, 0, 0)),
                pl.BlockSpec((attn.shape[0], tile), lambda i, m: (0, i)),
                whole(router_t.shape),
                whole(pick_row.shape),
                whole(back.shape),
            ],
            out_specs=pl.BlockSpec((tile, d), lambda i, m: (i, 0)),
        ),
        out_shape=jax.ShapeDtypeStruct((rows, d), BF),
        compiler_params=params(),
        cost_estimate=cost(2e9, 6e6),
        name="combine_pass",
    )(me, mixed, w_out, attn, router_t, pick_row, back)


def per_device(tokens, w_query, w_key, w_value, freq, w_out, router, w_in, w_down, picks):
    total, d = tokens.shape
    group = lax.axis_size("head")
    ring = lax.axis_size("seq")
    me = lax.axis_index("head")
    me_arr = jnp.stack([me, lax.axis_index("seq")]).astype(jnp.int32)
    rows = total // group
    experts, _, cap = picks.shape
    wid = w_query.shape[1]

    own = picks[:, 0, :]
    near = [own.T.reshape(1, cap * experts)]
    swap = lambda x, k: lax.ppermute(x, "head", [(i, i ^ k) for i in range(group)])
    near += [swap(near[0], k) for k in range(1, group)]
    pick_row = jnp.pad(own, ((0, 0), (0, PAD - cap)), constant_values=-1).reshape(1, experts * PAD)

    kf, vt, sc, state = key_pass(tokens, w_key.T, w_value.T, freq, rows, ring)
    states = lax.all_to_all(state, "seq", split_axis=0, concat_axis=0, tiled=True)
    qft, raw, seen = query_pass(me_arr, tokens, w_query.T, freq.T, kf, vt, sc, near)
    *attns, sent = norm_pass(me_arr, raw, qft, states, seen, near, cap)

    sent = sent.reshape(experts, group * cap, 2 * wid)
    arrived = lax.all_to_all(sent, ("seq", "head"), split_axis=0, concat_axis=0, tiled=True)
    early = [swap(attns[k], k) for k in range(1, group - 1)]
    arrived, *early = lax.optimization_barrier([arrived, *early])
    w_out = w_out.reshape(group, wid, d)
    result = expert_pass(
        arrived.reshape(ring, group, group * cap, 2 * wid), w_out, w_in, w_down, cap
    )
    back = lax.all_to_all(
        result.reshape(experts, PAD, d), ("seq", "head"), split_axis=0, concat_axis=0, tiled=True
    )
    late = swap(attns[-1], group - 1)
    mixed = mix_pass(me_arr, tokens, w_out, [attns[0], *early], rows)
    return combine_pass(
        me_arr, mixed, w_out, late, router.T, pick_row, back.reshape(experts * PAD, d)
    )


def solution(mesh):
    in_specs = (
        P("seq", None),
        P(None, "head"),
        P(None, "head"),
        P(None, "head"),
        P(),
        P(),
        P(),
        P(("seq", "head"), None, None),
        P(("seq", "head"), None, None),
        P(None, ("seq", "head"), None),
    )
    out_specs = P(("seq", "head"), None)
    return jax.shard_map(
        per_device, mesh=mesh, in_specs=in_specs, out_specs=out_specs, check_vma=False
    )
```

```python
import functools
import math

import jax
import jax.numpy as jnp
from jax import lax
from jax.experimental import pallas as pl
from jax.experimental.pallas import tpu as pltpu
from jax.sharding import PartitionSpec as P

HD = 64
EPS = 1e-06
CHUNK = 256
PAD = 8
BF = jnp.bfloat16
F32 = jnp.float32
MIB = 2**20
KEPT = 24
PIECES = ((0,), (1,), (2, 3))
SIN = (3.14158202, -5.16714279, 2.54189901, -0.55463616)
COS = (0.9999933, -4.93393802, 4.04128381, -1.22212701)


def nn(a, b):
    return lax.dot_general(a, b, (((1,), (0,)), ((), ())), preferred_element_type=F32)


def nt(a, b):
    return lax.dot_general(a, b, (((1,), (1,)), ((), ())), preferred_element_type=F32)


def tn(a, b):
    return lax.dot_general(a, b, (((0,), (0,)), ((), ())), preferred_element_type=F32)


def wave(turns, scale):
    big = F32(1.5 * 2.0**23)
    r = turns - ((turns + big) - big)
    u = r * r
    root = math.sqrt(2 * scale)
    a = [F32(v * root) for v in SIN]
    b = [F32(v * root) for v in COS]
    s = r * (a[0] + u * (a[1] + u * (a[2] + u * a[3])))
    c = b[0] + u * (b[1] + u * (b[2] + u * b[3]))
    return F32(scale) - s * s, s * c


def parts(f):
    hi = f.astype(BF)
    rest = f - hi.astype(F32)
    mid = rest.astype(BF)
    lo = (rest - mid.astype(F32)).astype(BF)
    return [hi, mid, lo]


def whole(shape):
    return pl.BlockSpec(shape, lambda *_: (0,) * len(shape))


def params(mib=60):
    return pltpu.CompilerParams(vmem_limit_bytes=mib * MIB)


def far(x):
    return pltpu.with_memory_space_constraint(x, pltpu.HBM)


def cost(flops, nbytes):
    return pl.CostEstimate(flops=int(flops), bytes_accessed=int(nbytes), transcendentals=0)


HERE = pl.BlockSpec(memory_space=pltpu.VMEM)
AWAY = pl.BlockSpec(memory_space=pl.ANY)
FAR = pl.BlockSpec(memory_space=pltpu.HBM)


def key_kernel(size, tok_hbm, wkt_hbm, wvt_hbm, freq_hbm, *rest):
    tok_ref, kf_ref, vt_ref, sc_ref, tot_ref, wkt_ref, wvt_ref, freq_ref, sems = rest
    total = tok_ref.shape[0]
    weights = [
        pltpu.make_async_copy(a, b, sems.at[i])
        for i, (a, b) in enumerate([(wkt_hbm, wkt_ref), (wvt_hbm, wvt_ref), (freq_hbm, freq_ref)])
    ]
    loads = [
        pltpu.make_async_copy(tok_hbm.at[pl.ds(first, size)], tok_ref.at[pl.ds(first, size)], sems.at[3 + i])
        for i, first in enumerate(range(0, total, size))
    ]
    for copy in [weights[0], loads[0], *weights[1:], *loads[1:]]:
        copy.start()
    for copy in weights:
        copy.wait()
    wid = wkt_ref.shape[0]
    heads = wid // HD
    half = freq_ref.shape[1]
    feat = 2 * half
    f3 = jnp.concatenate(parts(freq_ref[...] * F32(0.5 / math.pi)), axis=0)
    state = [jnp.zeros((HD, feat), F32) for _ in range(heads)]
    for first in range(0, total, size):
        span = slice(first, first + size)
        loads[first // size].wait()
        tok = tok_ref[span, :]
        k = nt(tok, wkt_ref[...]).astype(BF)
        vt = nt(wvt_ref[...], tok).astype(BF)
        vt_ref[:, span] = vt
        for h in range(heads):
            mine = slice(h * HD, (h + 1) * HD)
            phase = nn(jnp.concatenate([k[:, mine]] * 3, axis=1), f3)
            c, s = wave(phase, 1 / math.sqrt(half))
            kf = jnp.concatenate([c.astype(BF), s.astype(BF)], axis=1)
            kf_ref[span, h * feat : (h + 1) * feat] = kf
            for j in range(0, size, CHUNK):
                sc_ref[(first + j) // CHUNK, mine, :] = state[h].astype(BF)
                state[h] = state[h] + nn(vt[mine, j : j + CHUNK], kf[j : j + CHUNK])
    for h in range(heads):
        tot_ref[h * HD : (h + 1) * HD, :] = state[h].astype(BF)


def key_pass(tokens, wkt, wvt, freq, size):
    total, d = tokens.shape
    wid = wkt.shape[0]
    feat = 2 * freq.shape[1]
    heads = wid // HD
    return pl.pallas_call(
        functools.partial(key_kernel, size),
        in_specs=[FAR] * 4,
        out_specs=[HERE] * 5,
        out_shape=[
            jax.ShapeDtypeStruct(tokens.shape, BF),
            jax.ShapeDtypeStruct((total, heads * feat), BF),
            jax.ShapeDtypeStruct((wid, total), BF),
            jax.ShapeDtypeStruct((total // CHUNK, wid, feat), BF),
            jax.ShapeDtypeStruct((wid, feat), BF),
        ],
        scratch_shapes=[
            pltpu.VMEM(wkt.shape, BF),
            pltpu.VMEM(wvt.shape, BF),
            pltpu.VMEM(freq.shape, F32),
            pltpu.SemaphoreType.DMA((3 + total // size,)),
        ],
        compiler_params=params(KEPT),
        cost_estimate=cost(5e9, 12e6),
        name="key_pass",
    )(*map(far, (tokens, wkt, wvt, freq)))


def chosen(slot, pick_refs):
    row = pick_refs[0][...]
    for k in range(1, len(pick_refs)):
        row = jnp.where(slot == k, pick_refs[k][...], row)
    return row


def marks(row, rows):
    at = lax.broadcasted_iota(jnp.int32, (rows, row.shape[1]), 0)
    return (at == row).astype(F32).astype(BF)


def query_kernel(blocks, slots, tok_ref, wqt_ref, freq_ref, kf_ref, vt_ref, sc_ref, *rest):
    pick_refs = rest[:slots]
    qft_ref, raw_ref, seen_ref = rest[-3:]
    wid, d = wqt_ref.shape
    heads = wid // HD
    half = freq_ref.shape[1]
    feat = 2 * half
    rows = tok_ref.shape[0] // slots
    me = lax.axis_index("head")
    f3t = jnp.concatenate(parts(freq_ref[...].T * F32(0.5 / math.pi)), axis=1)
    line = lax.broadcasted_iota(jnp.int32, (wid, d), 0)
    column = lax.broadcasted_iota(jnp.int32, (wid, d), 1)
    both_w = jnp.concatenate([wqt_ref[...], (line + me * wid == column).astype(F32).astype(BF)], axis=0)
    place = [lax.broadcasted_iota(jnp.int32, (CHUNK, CHUNK), i) for i in (0, 1)]
    keep = place[0] <= place[1]
    for block in blocks:
        first = block * rows
        tok = tok_ref[first : first + rows, :]
        out = nt(both_w, tok).astype(BF)
        seen_ref[block] = nn(out[wid:], marks(chosen(me ^ block, pick_refs), rows)).astype(BF)
        for h in range(heads):
            mine = slice(h * HD, (h + 1) * HD)
            phase = nn(f3t, jnp.concatenate([out[mine]] * 3, axis=0))
            c, s = wave(phase, 1 / math.sqrt(half))
            qf = jnp.concatenate([c.astype(BF), s.astype(BF)], axis=0)
            qft_ref[block, h * feat : (h + 1) * feat, :] = qf
            for j in range(0, rows, CHUNK):
                cols = slice(j, j + CHUNK)
                there = slice(first + j, first + j + CHUNK)
                both = jnp.concatenate(
                    [kf_ref[there, h * feat : (h + 1) * feat], sc_ref[(first + j) // CHUNK, mine, :]], axis=0
                )
                both = nn(both, qf[:, cols])
                scores = jnp.where(keep, both[:CHUNK], 0.0).astype(BF)
                raw_ref[block, mine, cols] = nn(vt_ref[mine, there], scores) + both[CHUNK:]


def query_pass(blocks, tokens, wqt, freq, kf, vt, sc, picks, after, into):
    total, d = tokens.shape
    slots = len(picks)
    rows = total // slots
    n = picks[0].shape[1]
    wid = wqt.shape[0]
    feat = 2 * freq.shape[1]
    heads = wid // HD
    args = [tokens, wqt, freq, kf, vt, sc, *picks, after, *into]
    return pl.pallas_call(
        functools.partial(query_kernel, blocks, slots),
        in_specs=[HERE] * (len(args) - len(into) - 1) + [AWAY] * (len(into) + 1),
        out_specs=[HERE] * 3,
        out_shape=[
            jax.ShapeDtypeStruct((slots, heads * feat, rows), BF),
            jax.ShapeDtypeStruct((slots, wid, rows), F32),
            jax.ShapeDtypeStruct((slots, wid, n), BF),
        ],
        input_output_aliases={len(args) - len(into) + i: i for i in range(len(into))},
        compiler_params=params(KEPT),
        cost_estimate=cost(1.5e9 * len(blocks), 4e6 * len(blocks)),
        name="query_pass",
    )(*args)


def norm_kernel(slots, cap, rounds, raw_ref, qft_ref, seen_ref, *rest):
    got_refs, pick_refs = rest[:rounds], rest[rounds : rounds + slots]
    outs = rest[rounds + slots : rounds + 2 * slots]
    sent_hbm, ready, acc, sent, sems = rest[rounds + 2 * slots :]
    me, at = lax.axis_index("head"), lax.axis_index("seq")
    wid = raw_ref.shape[1]
    heads = wid // HD
    feat = got_refs[0].shape[1]
    before = jnp.zeros(got_refs[0].shape, F32)
    for i, got in enumerate(got_refs):
        before = before + jnp.where((at & (1 << i)) > 0, got[...].astype(F32), 0.0)
    before = before.astype(BF)
    copies = [pltpu.make_async_copy(ready.at[k], outs[k], sems.at[k]) for k in range(slots)]
    for k in range(slots):
        block = me ^ k
        for h in range(heads):
            mine = slice(h * HD, (h + 1) * HD)
            raw = raw_ref[block, mine, :] + nn(before[mine, :], qft_ref[block, h * feat : (h + 1) * feat, :])
            meansq = jnp.mean(raw * raw, axis=0, keepdims=True)
            ready[k, mine, :] = (raw * lax.rsqrt(meansq + F32(EPS))).astype(BF)
        copies[k].start()
        attn = ready[k]
        picked = nn(attn, marks(pick_refs[k][...], attn.shape[1])).astype(BF)
        both = jnp.concatenate([picked, seen_ref[block]], axis=0)
        n = both.shape[1]
        experts = n // cap
        entry = lax.broadcasted_iota(jnp.int32, (1, n), 1)
        row = (entry % experts * slots + block) * cap + entry // experts
        part = nt(marks(row, acc.shape[0]), both)
        acc[...] = part if k == 0 else acc[...] + part
    sent[...] = acc[...].astype(BF)
    last = pltpu.make_async_copy(sent, sent_hbm, sems.at[slots])
    last.start()
    for copy in copies:
        copy.wait()
    last.wait()


def norm_pass(raw, qft, seen, got, picks, cap):
    slots, wid, rows = raw.shape
    n = slots * picks[0].shape[1]
    return pl.pallas_call(
        functools.partial(norm_kernel, slots, cap, len(got)),
        in_specs=[HERE] * (3 + len(got) + slots),
        out_specs=[FAR] * (slots + 1),
        out_shape=[pltpu.HBM((wid, rows), BF)] * slots + [pltpu.HBM((n, 2 * wid), BF)],
        scratch_shapes=[
            pltpu.VMEM((slots, wid, rows), BF),
            pltpu.VMEM((n, 2 * wid), F32),
            pltpu.VMEM((n, 2 * wid), BF),
            pltpu.SemaphoreType.DMA((slots + 1,)),
        ],
        compiler_params=params(KEPT + n * wid * 20 // MIB),
        cost_estimate=cost(3e9, 8e6),
        name="norm_pass",
    )(raw, qft, seen, *got, *picks)


def expert_kernel(cap, tiles, got_hbm, wo_hbm, wi_hbm, wd_hbm, out_ref, got, wo, wi, wd, taken, acc, sems):
    slots, ring, each, both = got.shape
    wid = both // 2
    n, d = ring * each, wo.shape[2]
    ff = wi.shape[1]
    tile = ff // tiles
    landing = [pltpu.make_async_copy(got_hbm.at[:, h], got.at[h], sems.at[h]) for h in range(slots)]
    copies = [pltpu.make_async_copy(wo_hbm, wo, sems.at[slots])]
    first = slots + 1
    for t in range(tiles):
        cut = pl.ds(t * tile, tile)
        copies.append(pltpu.make_async_copy(wi_hbm.at[0, :, cut], wi.at[:, cut], sems.at[first + 2 * t]))
        copies.append(pltpu.make_async_copy(wd_hbm.at[0, cut, :], wd.at[cut, :], sems.at[first + 1 + 2 * t]))
    for c in landing + copies:
        c.start()
    for c in landing:
        c.wait()
    parts_in = [got[h].reshape(n, both) for h in range(slots)]
    mixed = jnp.concatenate([g.astype(F32)[:, wid:] for g in parts_in], axis=1)
    copies[0].wait()
    for h, g in enumerate(parts_in):
        mixed = mixed + nn(g[:, :wid], wo[h])
    taken[...] = mixed.astype(BF)
    acc[...] = jnp.zeros((n, d), F32)
    for t in range(tiles):
        cut = slice(t * tile, (t + 1) * tile)
        copies[1 + 2 * t].wait()
        inner = jax.nn.gelu(nn(taken[...], wi[:, cut]), approximate=True).astype(BF)
        copies[2 + 2 * t].wait()
        acc[...] += nn(inner, wd[cut, :])
    m = out_ref.shape[0]
    at = lax.broadcasted_iota(jnp.int32, (1, n), 1)
    out_ref[...] = nn(marks(at // cap * PAD + at % cap, m), acc[...].astype(BF)).astype(BF)


def expert_pass(arrived, w_out, w_in, w_down, cap, tiles=6):
    ring, slots, each, both = arrived.shape
    d, ff = w_in.shape[1:]
    m = ring * each // cap * PAD
    return pl.pallas_call(
        functools.partial(expert_kernel, cap, tiles),
        in_specs=[AWAY] + [FAR] * 3,
        out_specs=HERE,
        out_shape=jax.ShapeDtypeStruct((m, d), BF),
        scratch_shapes=[
            pltpu.VMEM((slots, ring, each, both), BF),
            pltpu.VMEM(w_out.shape, BF),
            pltpu.VMEM((d, ff), BF),
            pltpu.VMEM((ff, d), BF),
            pltpu.VMEM((ring * each, d), BF),
            pltpu.VMEM((ring * each, d), F32),
            pltpu.SemaphoreType.DMA((slots + 1 + 2 * tiles,)),
        ],
        compiler_params=params(40),
        cost_estimate=cost(2e9, 12e6),
        name="expert_pass",
    )(arrived, *map(far, (w_out, w_in, w_down)))


def mix_kernel(slots, me_ref, tok_ref, wo_ref, *rest):
    attns, out_ref = rest[:-1], rest[-1]
    mixed = tok_ref[...].astype(F32)
    for k in slots:
        mixed = mixed + tn(attns[k][...], wo_ref[me_ref[0] ^ k])
    out_ref[...] = mixed


def mix_pass(me, tokens, w_out, attns, rows):
    d = tokens.shape[1]
    return pl.pallas_call(
        functools.partial(mix_kernel, range(len(attns))),
        grid_spec=pltpu.PrefetchScalarGridSpec(
            num_scalar_prefetch=1,
            grid=(1,),
            in_specs=[pl.BlockSpec((rows, d), lambda i, m: (m[0], 0)), whole(w_out.shape)]
            + [whole(a.shape) for a in attns],
            out_specs=whole((rows, d)),
        ),
        out_shape=jax.ShapeDtypeStruct((rows, d), F32),
        compiler_params=params(),
        cost_estimate=cost(2e9, 6e6),
        name="mix_pass",
    )(me, tokens, w_out, *attns)


def combine_kernel(me_ref, mix_ref, wo_ref, attn_ref, router_ref, pick_ref, back_ref, out_ref):
    hidden = (mix_ref[...] + tn(attn_ref[...], wo_ref[0])).astype(BF)
    gate = jax.nn.sigmoid(nt(hidden, router_ref[...])).astype(BF)
    e, n = gate.shape[1], pick_ref.shape[1]
    rows = hidden.shape[0]
    source = lax.broadcasted_iota(jnp.int32, (1, n), 1) // PAD
    spread = nn(gate, marks(source, e))
    at = lax.broadcasted_iota(jnp.int32, (rows, n), 0) + pl.program_id(0) * rows
    comb = jnp.where(pick_ref[...] == at, spread, 0.0).astype(BF)
    out_ref[...] = (hidden.astype(F32) + nn(comb, back_ref[...])).astype(BF)


def combine_pass(me, mixed, w_out, attn, router_t, pick_row, back, tiles=3):
    rows, d = mixed.shape
    last = w_out.shape[0] - 1
    tile = rows // tiles
    return pl.pallas_call(
        combine_kernel,
        grid_spec=pltpu.PrefetchScalarGridSpec(
            num_scalar_prefetch=1,
            grid=(tiles,),
            in_specs=[
                pl.BlockSpec((tile, d), lambda i, m: (i, 0)),
                pl.BlockSpec((1,) + w_out.shape[1:], lambda i, m: (m[0] ^ last, 0, 0)),
                pl.BlockSpec((attn.shape[0], tile), lambda i, m: (0, i)),
                whole(router_t.shape),
                whole(pick_row.shape),
                whole(back.shape),
            ],
            out_specs=pl.BlockSpec((tile, d), lambda i, m: (i, 0)),
        ),
        out_shape=jax.ShapeDtypeStruct((rows, d), BF),
        compiler_params=params(),
        cost_estimate=cost(2e9, 6e6),
        name="combine_pass",
    )(me, mixed, w_out, attn, router_t, pick_row, back)


def per_device(tokens, w_query, w_key, w_value, freq, w_out, router, w_in, w_down, picks):
    total, d = tokens.shape
    group = lax.axis_size("head")
    ring = lax.axis_size("seq")
    me = lax.axis_index("head")
    me_arr = jnp.stack([me, lax.axis_index("seq")]).astype(jnp.int32)
    rows = total // group
    experts, _, cap = picks.shape
    wid = w_query.shape[1]

    own = picks[:, 0, :]
    near = [own.T.reshape(1, cap * experts)]
    swap = lambda x, k: lax.ppermute(x, "head", [(i, i ^ k) for i in range(group)])
    near += [swap(near[0], k) for k in range(1, group)]
    pick_row = jnp.pad(own, ((0, 0), (0, PAD - cap)), constant_values=-1).reshape(1, experts * PAD)

    tok_here, kf, vt, sc, held = key_pass(tokens, w_key.T, w_value.T, freq, rows)
    got = []
    made = []
    stride = 1
    while stride < ring:
        last = 2 * stride >= ring
        pairs = [(i, i ^ stride) for i in range(ring) if not last or i & stride == 0]
        got.append(lax.ppermute(held, "seq", pairs))
        blocks = PIECES[len(got) - 1] if len(got) <= len(PIECES) else ()
        if blocks:
            made = query_pass(blocks, tok_here, w_query.T, freq, kf, vt, sc, near, held, made)
        held = (held.astype(F32) + got[-1].astype(F32)).astype(BF)
        stride *= 2
    qft, raw, seen = made
    *attns, sent = norm_pass(raw, qft, seen, got, near, cap)

    sent = sent.reshape(experts, group * cap, 2 * wid)
    arrived = lax.all_to_all(sent, ("seq", "head"), split_axis=0, concat_axis=0, tiled=True)
    early = [swap(attns[k], k) for k in range(1, group - 1)]
    arrived, *early = lax.optimization_barrier([arrived, *early])
    w_out = w_out.reshape(group, wid, d)
    result = expert_pass(
        arrived.reshape(ring, group, group * cap, 2 * wid), w_out, w_in, w_down, cap
    )
    back = lax.all_to_all(
        result.reshape(experts, PAD, d), ("seq", "head"), split_axis=0, concat_axis=0, tiled=True
    )
    late = swap(attns[-1], group - 1)
    mixed = mix_pass(me_arr, tokens, w_out, [attns[0], *early], rows)
    return combine_pass(
        me_arr, mixed, w_out, late, router.T, pick_row, back.reshape(experts * PAD, d)
    )


def solution(mesh):
    in_specs = (
        P("seq", None),
        P(None, "head"),
        P(None, "head"),
        P(None, "head"),
        P(),
        P(),
        P(),
        P(("seq", "head"), None, None),
        P(("seq", "head"), None, None),
        P(None, ("seq", "head"), None),
    )
    out_specs = P(("seq", "head"), None)
    return jax.shard_map(
        per_device, mesh=mesh, in_specs=in_specs, out_specs=out_specs, check_vma=False
    )
```

```python
import functools
import math

import jax
import jax.numpy as jnp
from jax import lax
from jax.experimental import pallas as pl
from jax.experimental.pallas import tpu as pltpu
from jax.sharding import PartitionSpec as P

HD = 64
EPS = 1e-06
CHUNK = 256
PAD = 8
BF = jnp.bfloat16
F32 = jnp.float32
MIB = 2**20
KEPT = 24
LANES = 128
SIN = (3.14158202, -5.16714279, 2.54189901, -0.55463616)
COS = (0.9999933, -4.93393802, 4.04128381, -1.22212701)


def nn(a, b):
    return lax.dot_general(a, b, (((1,), (0,)), ((), ())), preferred_element_type=F32)


def nt(a, b):
    return lax.dot_general(a, b, (((1,), (1,)), ((), ())), preferred_element_type=F32)


def tn(a, b):
    return lax.dot_general(a, b, (((0,), (0,)), ((), ())), preferred_element_type=F32)


def wave(turns, scale):
    big = F32(1.5 * 2.0**23)
    r = turns - ((turns + big) - big)
    u = r * r
    root = math.sqrt(2 * scale)
    a = [F32(v * root) for v in SIN]
    b = [F32(v * root) for v in COS]
    s = r * (a[0] + u * (a[1] + u * (a[2] + u * a[3])))
    c = b[0] + u * (b[1] + u * (b[2] + u * b[3]))
    return F32(scale) - s * s, s * c


def parts(f):
    hi = f.astype(BF)
    rest = f - hi.astype(F32)
    mid = rest.astype(BF)
    lo = (rest - mid.astype(F32)).astype(BF)
    return [hi, mid, lo]


def whole(shape):
    return pl.BlockSpec(shape, lambda *_: (0,) * len(shape))


def params(mib=60):
    return pltpu.CompilerParams(vmem_limit_bytes=mib * MIB)


def far(x):
    return pltpu.with_memory_space_constraint(x, pltpu.HBM)


def cost(flops, nbytes):
    return pl.CostEstimate(flops=int(flops), bytes_accessed=int(nbytes), transcendentals=0)


HERE = pl.BlockSpec(memory_space=pltpu.VMEM)
AWAY = pl.BlockSpec(memory_space=pl.ANY)
FAR = pl.BlockSpec(memory_space=pltpu.HBM)


def key_kernel(size, tok_hbm, wkt_hbm, wvt_hbm, freq_hbm, pick_ref, *rest):
    tok_ref, kf_ref, vt_ref, sc_ref, tot_ref, own_ref, w_ref, freq_ref, sems = rest
    total = tok_ref.shape[0]
    wid = wkt_hbm.shape[0]
    heads = wid // HD
    half = freq_ref.shape[1]
    feat = 2 * half
    count = total // size
    weights = [
        pltpu.make_async_copy(w, w_ref.at[pl.ds(i * wid, wid)], sems.at[i])
        for i, w in enumerate((wkt_hbm, wvt_hbm))
    ]
    weights.append(pltpu.make_async_copy(freq_hbm, freq_ref, sems.at[2]))
    loads = [
        pltpu.make_async_copy(
            tok_hbm.at[pl.ds(i * size, size)], tok_ref.at[pl.ds(i * size, size)], sems.at[3 + i]
        )
        for i in range(count)
    ]
    for copy in [weights[0], loads[0], *weights[1:], *loads[1:]]:
        copy.start()
    for copy in weights:
        copy.wait()
    f3 = jnp.concatenate(parts(freq_ref[...] * F32(0.5 / math.pi)), axis=0)
    state = [jnp.zeros((HD, feat), F32) for _ in range(heads)]
    units = [(i, j, h) for i in range(count) for j in range(0, size, CHUNK) for h in range(heads)]
    per = len(units) // count
    key, val, phase, feats = {}, {}, {}, {}

    def project(i):
        loads[i].wait()
        span = slice(i * size, (i + 1) * size)
        out = nt(tok_ref[span, :], w_ref[...]).astype(BF)
        key[i] = out[:, :wid]
        val[i] = out[:, wid:].T
        vt_ref[:, span] = val[i]

    def turn(u):
        i, j, h = u
        k = key[i][j : j + CHUNK, h * HD : (h + 1) * HD]
        phase[u] = nn(jnp.concatenate([k] * 3, axis=1), f3)

    def feature(u):
        i, j, h = u
        c, s = wave(phase.pop(u), 1 / math.sqrt(half))
        feats[u] = jnp.concatenate([c.astype(BF), s.astype(BF)], axis=1)
        kf_ref[i * size + j : i * size + j + CHUNK, h * feat : (h + 1) * feat] = feats[u]

    def gather(u):
        i, j, h = u
        mine = slice(h * HD, (h + 1) * HD)
        sc_ref[(i * size + j) // CHUNK, mine, :] = state[h].astype(BF)
        state[h] = state[h] + nn(val[i][mine, j : j + CHUNK], feats.pop(u))

    project(0)
    for t in range(len(units) + 2):
        if t % per == per // 2 and t // per + 1 < count:
            project(t // per + 1)
        if t < len(units):
            turn(units[t])
        if 0 <= t - 1 < len(units):
            feature(units[t - 1])
        if 0 <= t - 2 < len(units):
            gather(units[t - 2])
    for h in range(heads):
        tot_ref[h * HD : (h + 1) * HD, :] = state[h].astype(BF)
    own_ref[...] = jnp.concatenate([pick_ref[c] for c in range(pick_ref.shape[0])], axis=1)


def key_pass(tokens, wkt, wvt, freq, picks, size):
    total, d = tokens.shape
    wid = wkt.shape[0]
    feat = 2 * freq.shape[1]
    heads = wid // HD
    return pl.pallas_call(
        functools.partial(key_kernel, size),
        in_specs=[FAR] * 4 + [HERE],
        out_specs=[HERE] * 6,
        out_shape=[
            jax.ShapeDtypeStruct(tokens.shape, BF),
            jax.ShapeDtypeStruct((total, heads * feat), BF),
            jax.ShapeDtypeStruct((wid, total), BF),
            jax.ShapeDtypeStruct((total // CHUNK, wid, feat), BF),
            jax.ShapeDtypeStruct((wid, feat), BF),
            jax.ShapeDtypeStruct((1, picks.size), jnp.int32),
        ],
        scratch_shapes=[
            pltpu.VMEM((2 * wid, d), BF),
            pltpu.VMEM(freq.shape, F32),
            pltpu.SemaphoreType.DMA((3 + total // size,)),
        ],
        compiler_params=params(KEPT),
        cost_estimate=cost(5e9, 12e6),
        name="key_pass",
    )(*map(far, (tokens, wkt, wvt, freq)), picks)


def chosen(slot, pick_refs):
    row = pick_refs[0][...]
    for k in range(1, len(pick_refs)):
        row = jnp.where(slot == k, pick_refs[k][...], row)
    return row


def marks(row, rows):
    at = lax.broadcasted_iota(jnp.int32, (rows, row.shape[1]), 0)
    return (at == row).astype(F32).astype(BF)


def query_kernel(chunks, slots, picked, tok_ref, freq_ref, wqt_ref, kf_ref, vt_ref, sc_ref, *rest):
    pick_refs = rest[:picked]
    qft_ref, raw_ref = rest[-2 - (picked > 0) :][:2]
    wid = wqt_ref.shape[0]
    heads = wid // HD
    half = freq_ref.shape[1]
    feat = 2 * half
    rows = tok_ref.shape[0] // slots
    me = lax.axis_index("head")
    f3t = jnp.concatenate(parts(freq_ref[...].T * F32(0.5 / math.pi)), axis=1)
    place = [lax.broadcasted_iota(jnp.int32, (CHUNK, CHUNK), i) for i in (0, 1)]
    keep = place[0] <= place[1]
    units = [(c * CHUNK // rows, c * CHUNK % rows, h) for c in chunks for h in range(heads)]
    base = chunks[0] * CHUNK
    span = slice(base, base + len(chunks) * CHUNK)
    query = nt(tok_ref[span, :], wqt_ref[...]).astype(BF).T
    phase, feats, both = {}, {}, {}

    def spot(u):
        b, j, h = u
        return slice(h * HD, (h + 1) * HD), slice(b * rows + j, b * rows + j + CHUNK), slice(h * feat, (h + 1) * feat)

    def select(b):
        span = slice(b * rows, (b + 1) * rows)
        start = me * wid
        wide = -(-wid // LANES) * LANES
        low = pl.multiple_of(start // LANES * LANES, LANES)
        window = tok_ref[span, pl.ds(low, wide)]
        columns = window[:, :wid]
        for shift in range(math.gcd(wid, LANES), wide - wid + 1, math.gcd(wid, LANES)):
            columns = jnp.where(start % LANES == shift, window[:, shift : shift + wid], columns)
        rest[-1][b] = tn(columns, marks(chosen(me ^ b, pick_refs), rows)).astype(BF)

    def turn(u):
        mine, cols, _ = spot(u)
        q = query[mine, cols.start - base : cols.stop - base]
        phase[u] = nn(f3t, jnp.concatenate([q] * 3, axis=0))

    def feature(u):
        b, j, h = u
        c, s = wave(phase.pop(u), 1 / math.sqrt(half))
        feats[u] = jnp.concatenate([c.astype(BF), s.astype(BF)], axis=0)
        qft_ref[b, h * feat : (h + 1) * feat, j : j + CHUNK] = feats[u]

    def score(u):
        mine, cols, lines = spot(u)
        keys = jnp.concatenate([kf_ref[cols, lines], sc_ref[cols.start // CHUNK, mine, :]], axis=0)
        both[u] = nn(keys, feats.pop(u))

    def total(u):
        b, j, h = u
        mine, cols, _ = spot(u)
        got = both.pop(u)
        scores = jnp.where(keep, got[:CHUNK], 0.0).astype(BF)
        raw_ref[b, mine, j : j + CHUNK] = nn(vt_ref[mine, cols], scores) + got[CHUNK:]

    stages = (turn, feature, score, total)
    lag = 2
    for t in range(len(units) + lag * (len(stages) - 1)):
        if picked and t % heads == heads - 1 and t // heads < slots:
            select(t // heads)
        for i, stage in enumerate(stages):
            if 0 <= t - lag * i < len(units):
                stage(units[t - lag * i])


def query_pass(chunks, tokens, freq, wqt, kf, vt, sc, picks, slots, into):
    total, d = tokens.shape
    rows = total // slots
    wid = wqt.shape[0]
    feat = 2 * freq.shape[1]
    heads = wid // HD
    out_shape = [
        jax.ShapeDtypeStruct((slots, heads * feat, rows), BF),
        jax.ShapeDtypeStruct((slots, wid, rows), F32),
    ]
    if picks:
        out_shape.append(jax.ShapeDtypeStruct((slots, wid, picks[0].shape[1]), BF))
    args = [tokens, freq, wqt, kf, vt, sc, *picks, *into]
    return pl.pallas_call(
        functools.partial(query_kernel, chunks, slots, len(picks)),
        in_specs=[HERE] * (len(args) - len(into)) + [AWAY] * len(into),
        out_specs=[HERE] * len(out_shape),
        out_shape=out_shape,
        input_output_aliases={len(args) - len(into) + i: i for i in range(2) if into},
        compiler_params=params(KEPT),
        cost_estimate=cost(5e8 * len(chunks), 1e6 * len(chunks)),
        name="query_pass",
    )(*args)


def norm_kernel(slots, cap, rounds, raw_ref, qft_ref, seen_ref, *rest):
    got_refs, pick_refs = rest[:rounds], rest[rounds : rounds + slots]
    outs = rest[rounds + slots : rounds + 2 * slots]
    sent_hbm, ready, acc, sent, sems = rest[rounds + 2 * slots :]
    me, at = lax.axis_index("head"), lax.axis_index("seq")
    wid = raw_ref.shape[1]
    heads = wid // HD
    feat = got_refs[0].shape[1]
    before = jnp.zeros(got_refs[0].shape, F32)
    for i, got in enumerate(got_refs):
        before = before + jnp.where((at & (1 << i)) > 0, got[...].astype(F32), 0.0)
    before = before.astype(BF)
    copies = [pltpu.make_async_copy(ready.at[k], outs[k], sems.at[k]) for k in range(slots)]
    picked = {}

    def norm(k):
        block = me ^ k
        for h in range(heads):
            mine = slice(h * HD, (h + 1) * HD)
            raw = raw_ref[block, mine, :] + nn(before[mine, :], qft_ref[block, h * feat : (h + 1) * feat, :])
            meansq = jnp.mean(raw * raw, axis=0, keepdims=True)
            ready[k, mine, :] = (raw * lax.rsqrt(meansq + F32(EPS))).astype(BF)
        copies[k].start()

    def pick(k):
        picked[k] = nn(ready[k], marks(pick_refs[k][...], ready.shape[2])).astype(BF)

    def spread(k):
        both = jnp.concatenate([picked.pop(k), seen_ref[me ^ k]], axis=0)
        n = both.shape[1]
        experts = n // cap
        entry = lax.broadcasted_iota(jnp.int32, (1, n), 1)
        row = (entry % experts * slots + (me ^ k)) * cap + entry // experts
        part = nt(marks(row, acc.shape[0]), both)
        acc[...] = part if k == 0 else acc[...] + part

    stages = (norm, pick, spread)
    for t in range(slots + len(stages) - 1):
        for i, stage in enumerate(stages):
            if 0 <= t - i < slots:
                stage(t - i)
    sent[...] = acc[...].astype(BF)
    last = pltpu.make_async_copy(sent, sent_hbm, sems.at[slots])
    last.start()
    for copy in copies:
        copy.wait()
    last.wait()


def norm_pass(raw, qft, seen, got, picks, cap):
    slots, wid, rows = raw.shape
    n = slots * picks[0].shape[1]
    return pl.pallas_call(
        functools.partial(norm_kernel, slots, cap, len(got)),
        in_specs=[HERE] * (3 + len(got) + slots),
        out_specs=[FAR] * (slots + 1),
        out_shape=[pltpu.HBM((wid, rows), BF)] * slots + [pltpu.HBM((n, 2 * wid), BF)],
        scratch_shapes=[
            pltpu.VMEM((slots, wid, rows), BF),
            pltpu.VMEM((n, 2 * wid), F32),
            pltpu.VMEM((n, 2 * wid), BF),
            pltpu.SemaphoreType.DMA((slots + 1,)),
        ],
        compiler_params=params(KEPT + n * wid * 20 // MIB),
        cost_estimate=cost(3e9, 8e6),
        name="norm_pass",
    )(raw, qft, seen, *got, *picks)


def expert_kernel(cap, tiles, got_hbm, wo_hbm, wi_hbm, wd_hbm, out_ref, got, wo, wi, wd, taken, acc, sems):
    slots, ring, each, both = got.shape
    wid = both // 2
    n, d = ring * each, wo.shape[2]
    ff = wi.shape[1]
    tile = ff // tiles
    landing = [pltpu.make_async_copy(got_hbm.at[:, h], got.at[h], sems.at[h]) for h in range(slots)]
    copies = [pltpu.make_async_copy(wo_hbm, wo, sems.at[slots])]
    first = slots + 1
    for t in range(tiles):
        cut = pl.ds(t * tile, tile)
        copies.append(pltpu.make_async_copy(wi_hbm.at[0, :, cut], wi.at[:, cut], sems.at[first + 2 * t]))
        copies.append(pltpu.make_async_copy(wd_hbm.at[0, cut, :], wd.at[cut, :], sems.at[first + 1 + 2 * t]))
    for c in landing + copies:
        c.start()
    for c in landing:
        c.wait()
    parts_in = [got[h].reshape(n, both) for h in range(slots)]
    mixed = jnp.concatenate([g.astype(F32)[:, wid:] for g in parts_in], axis=1)
    copies[0].wait()
    for h, g in enumerate(parts_in):
        mixed = mixed + nn(g[:, :wid], wo[h])
    taken[...] = mixed.astype(BF)
    acc[...] = jnp.zeros((n, d), F32)
    for t in range(tiles):
        cut = slice(t * tile, (t + 1) * tile)
        copies[1 + 2 * t].wait()
        inner = jax.nn.gelu(nn(taken[...], wi[:, cut]), approximate=True).astype(BF)
        copies[2 + 2 * t].wait()
        acc[...] += nn(inner, wd[cut, :])
    m = out_ref.shape[0]
    at = lax.broadcasted_iota(jnp.int32, (1, n), 1)
    out_ref[...] = nn(marks(at // cap * PAD + at % cap, m), acc[...].astype(BF)).astype(BF)


def expert_pass(arrived, w_out, w_in, w_down, cap, tiles=3):
    ring, slots, each, both = arrived.shape
    d, ff = w_in.shape[1:]
    m = ring * each // cap * PAD
    return pl.pallas_call(
        functools.partial(expert_kernel, cap, tiles),
        in_specs=[AWAY] + [FAR] * 3,
        out_specs=HERE,
        out_shape=jax.ShapeDtypeStruct((m, d), BF),
        scratch_shapes=[
            pltpu.VMEM((slots, ring, each, both), BF),
            pltpu.VMEM(w_out.shape, BF),
            pltpu.VMEM((d, ff), BF),
            pltpu.VMEM((ff, d), BF),
            pltpu.VMEM((ring * each, d), BF),
            pltpu.VMEM((ring * each, d), F32),
            pltpu.SemaphoreType.DMA((slots + 1 + 2 * tiles,)),
        ],
        compiler_params=params(40),
        cost_estimate=cost(2e9, 12e6),
        name="expert_pass",
    )(arrived, *map(far, (w_out, w_in, w_down)))


def mix_kernel(slots, tok_hbm, wo_hbm, *rest):
    attns, (out_ref, tok, wo, sems) = rest[:-4], rest[-4:]
    me = lax.axis_index("head")
    rows = tok.shape[0]
    first = pl.multiple_of(me * rows, rows)
    copies = [pltpu.make_async_copy(tok_hbm.at[pl.ds(first, rows)], tok, sems.at[0])]
    copies += [pltpu.make_async_copy(wo_hbm.at[me ^ k], wo.at[k], sems.at[1 + k]) for k in range(slots)]
    for copy in copies:
        copy.start()
    for copy in copies:
        copy.wait()
    mixed = tok[...].astype(F32)
    for k in range(slots):
        mixed = mixed + tn(attns[k][...], wo[k])
    out_ref[...] = mixed


def mix_pass(tokens, w_out, attns, rows):
    d = tokens.shape[1]
    slots = len(attns)
    return pl.pallas_call(
        functools.partial(mix_kernel, slots),
        in_specs=[FAR] * 2 + [HERE] * slots,
        out_specs=HERE,
        out_shape=jax.ShapeDtypeStruct((rows, d), F32),
        scratch_shapes=[
            pltpu.VMEM((rows, d), BF),
            pltpu.VMEM((slots,) + w_out.shape[1:], BF),
            pltpu.SemaphoreType.DMA((1 + slots,)),
        ],
        compiler_params=params(),
        cost_estimate=cost(2e9, 6e6),
        name="mix_pass",
    )(far(tokens), far(w_out), *attns)


def combine_kernel(last, tiles, mix_hbm, wo_hbm, attn_hbm, router_ref, pick_ref, back_hbm, out_hbm, *scratch):
    mix, wo, attn, back, out, in_sems, out_sems = scratch
    me = lax.axis_index("head")
    rows = mix.shape[0]
    tile = rows // tiles
    cuts = [pl.ds(t * tile, tile) for t in range(tiles)]
    need = [
        pltpu.make_async_copy(wo_hbm.at[me ^ last], wo, in_sems.at[0]),
        pltpu.make_async_copy(attn_hbm, attn, in_sems.at[1]),
    ]
    later = pltpu.make_async_copy(back_hbm, back, in_sems.at[2])
    loads = [pltpu.make_async_copy(mix_hbm.at[c], mix.at[c], in_sems.at[3 + t]) for t, c in enumerate(cuts)]
    stores = [pltpu.make_async_copy(out.at[c], out_hbm.at[c], out_sems.at[t]) for t, c in enumerate(cuts)]
    for copy in [*need, loads[0], later, *loads[1:]]:
        copy.start()
    for copy in need:
        copy.wait()
    experts, n = router_ref.shape[0], pick_ref.shape[1]
    spreads = marks(lax.broadcasted_iota(jnp.int32, (1, n), 1) // PAD, experts)
    for t, cut in enumerate(cuts):
        loads[t].wait()
        hidden = (mix[cut, :] + tn(attn[:, t * tile : (t + 1) * tile], wo[...])).astype(BF)
        gate = jax.nn.sigmoid(nt(hidden, router_ref[...])).astype(BF)
        at = lax.broadcasted_iota(jnp.int32, (tile, n), 0) + t * tile
        comb = jnp.where(pick_ref[...] == at, nn(gate, spreads), 0.0).astype(BF)
        if t == 0:
            later.wait()
        out[cut, :] = (hidden.astype(F32) + nn(comb, back[...])).astype(BF)
        stores[t].start()
    for store in stores:
        store.wait()


def combine_pass(mixed, w_out, attn, router_t, pick_row, back, tiles=2):
    rows, d = mixed.shape
    last = w_out.shape[0] - 1
    return pl.pallas_call(
        functools.partial(combine_kernel, last, tiles),
        in_specs=[FAR, FAR, AWAY, HERE, HERE, AWAY],
        out_specs=AWAY,
        out_shape=jax.ShapeDtypeStruct((rows, d), BF),
        scratch_shapes=[
            pltpu.VMEM((rows, d), F32),
            pltpu.VMEM(w_out.shape[1:], BF),
            pltpu.VMEM(attn.shape, BF),
            pltpu.VMEM(back.shape, BF),
            pltpu.VMEM((rows, d), BF),
            pltpu.SemaphoreType.DMA((3 + tiles,)),
            pltpu.SemaphoreType.DMA((tiles,)),
        ],
        compiler_params=params(40),
        cost_estimate=cost(2e9, 6e6),
        name="combine_pass",
    )(far(mixed), far(w_out), attn, router_t, pick_row, back)


def per_device(tokens, w_query, w_key, w_value, freq, w_out, router, w_in, w_down, picks):
    total, d = tokens.shape
    group = lax.axis_size("head")
    ring = lax.axis_size("seq")
    rows = total // group
    experts, _, cap = picks.shape
    wid = w_query.shape[1]

    pick_row = jnp.pad(picks[:, 0, :], ((0, 0), (0, PAD - cap)), constant_values=-1).reshape(1, experts * PAD)
    swap = lambda x, k: lax.ppermute(x, "head", [(i, i ^ k) for i in range(group)])

    tok_here, kf, vt, sc, held, own = key_pass(
        tokens, w_key.T, w_value.T, freq, picks.transpose(2, 1, 0), rows
    )
    near = [own] + [swap(own, k) for k in range(1, group)]
    got, made = [], []
    chunks = total // CHUNK
    rounds = ring.bit_length() - 1
    for i in range(rounds):
        got.append(lax.ppermute(held, "seq", [(j, j ^ (1 << i)) for j in range(ring)]))
        part = range(chunks * i // rounds, chunks * (i + 1) // rounds)
        made = query_pass(
            part, tok_here, freq, w_query.T, kf, vt, sc, near if i == rounds - 1 else [], group, made
        )
        both = held.astype(F32) + got[-1].astype(F32)
        held, *made = lax.optimization_barrier([both.astype(BF), *made])
    qft, raw, seen = made
    *attns, sent = norm_pass(raw, qft, seen, got, near, cap)

    sent = sent.reshape(experts, group * cap, 2 * wid)
    arrived = lax.all_to_all(sent, ("seq", "head"), split_axis=0, concat_axis=0, tiled=True)
    early = [swap(attns[k], k) for k in range(1, group - 1)]
    arrived, pick_row, *early = lax.optimization_barrier([arrived, pick_row, *early])
    w_out = w_out.reshape(group, wid, d)
    result = expert_pass(
        arrived.reshape(ring, group, group * cap, 2 * wid), w_out, w_in, w_down, cap
    )
    back = lax.all_to_all(
        result.reshape(experts, PAD, d), ("seq", "head"), split_axis=0, concat_axis=0, tiled=True
    )
    late = swap(attns[-1], group - 1)
    mixed = mix_pass(tokens, w_out, [attns[0], *early], rows)
    return combine_pass(
        mixed, w_out, late, router.T, pick_row, back.reshape(experts * PAD, d)
    )


def solution(mesh):
    in_specs = (
        P("seq", None),
        P(None, "head"),
        P(None, "head"),
        P(None, "head"),
        P(),
        P(),
        P(),
        P(("seq", "head"), None, None),
        P(("seq", "head"), None, None),
        P(None, ("seq", "head"), None),
    )
    out_specs = P(("seq", "head"), None)
    return jax.shard_map(
        per_device, mesh=mesh, in_specs=in_specs, out_specs=out_specs, check_vma=False
    )
```

```python
import functools
import math

import jax
import jax.numpy as jnp
from jax import lax
from jax.experimental import pallas as pl
from jax.experimental.pallas import tpu as pltpu
from jax.sharding import PartitionSpec as P

HD = 64
EPS = 1e-06
CHUNK = 256
PAD = 8
BF = jnp.bfloat16
F32 = jnp.float32
MIB = 2**20
KEPT = 24
LANES = 128
SIN = (3.14158202, -5.16714279, 2.54189901, -0.55463616)
COS = (0.9999933, -4.93393802, 4.04128381, -1.22212701)


def nn(a, b):
    return lax.dot_general(a, b, (((1,), (0,)), ((), ())), preferred_element_type=F32)


def nt(a, b):
    return lax.dot_general(a, b, (((1,), (1,)), ((), ())), preferred_element_type=F32)


def tn(a, b):
    return lax.dot_general(a, b, (((0,), (0,)), ((), ())), preferred_element_type=F32)


def wave(turns, scale):
    big = F32(1.5 * 2.0**23)
    r = turns - ((turns + big) - big)
    u = r * r
    root = math.sqrt(2 * scale)
    a = [F32(v * root) for v in SIN]
    b = [F32(v * root) for v in COS]
    s = r * (a[0] + u * (a[1] + u * (a[2] + u * a[3])))
    c = b[0] + u * (b[1] + u * (b[2] + u * b[3]))
    return F32(scale) - s * s, s * c


def parts(f):
    hi = f.astype(BF)
    rest = f - hi.astype(F32)
    mid = rest.astype(BF)
    lo = (rest - mid.astype(F32)).astype(BF)
    return [hi, mid, lo]


def whole(shape):
    return pl.BlockSpec(shape, lambda *_: (0,) * len(shape))


def params(mib=60):
    return pltpu.CompilerParams(vmem_limit_bytes=mib * MIB)


def far(x):
    return pltpu.with_memory_space_constraint(x, pltpu.HBM)


def cost(flops, nbytes):
    return pl.CostEstimate(flops=int(flops), bytes_accessed=int(nbytes), transcendentals=0)


HERE = pl.BlockSpec(memory_space=pltpu.VMEM)
AWAY = pl.BlockSpec(memory_space=pl.ANY)
FAR = pl.BlockSpec(memory_space=pltpu.HBM)


def key_kernel(size, tok_hbm, wkt_hbm, wvt_hbm, freq_hbm, pick_hbm, *rest):
    tok_ref, kf_ref, vt_ref, sc_ref, tot_ref, own_ref, w_ref, freq_ref, pick_ref, sems = rest
    total = tok_ref.shape[0]
    wid = wkt_hbm.shape[0]
    heads = wid // HD
    half = freq_ref.shape[1]
    feat = 2 * half
    count = total // size
    weights = [
        pltpu.make_async_copy(w, w_ref.at[pl.ds(i * wid, wid)], sems.at[i])
        for i, w in enumerate((wkt_hbm, wvt_hbm))
    ]
    weights.append(pltpu.make_async_copy(freq_hbm, freq_ref, sems.at[2]))
    weights.append(pltpu.make_async_copy(pick_hbm, pick_ref, sems.at[3]))
    loads = [
        pltpu.make_async_copy(
            tok_hbm.at[pl.ds(i * size, size)], tok_ref.at[pl.ds(i * size, size)], sems.at[4 + i]
        )
        for i in range(count)
    ]
    for copy in [weights[0], loads[0], *weights[1:], *loads[1:]]:
        copy.start()
    for copy in weights:
        copy.wait()
    f3 = jnp.concatenate(parts(freq_ref[...] * F32(0.5 / math.pi)), axis=0)
    state = [jnp.zeros((HD, feat), F32) for _ in range(heads)]
    units = [(i, j, h) for i in range(count) for j in range(0, size, CHUNK) for h in range(heads)]
    per = len(units) // count
    key, val, phase, feats = {}, {}, {}, {}

    def project(i):
        loads[i].wait()
        span = slice(i * size, (i + 1) * size)
        out = nt(tok_ref[span, :], w_ref[...]).astype(BF)
        key[i] = out[:, :wid]
        val[i] = out[:, wid:].T
        vt_ref[:, span] = val[i]

    def turn(u):
        i, j, h = u
        k = key[i][j : j + CHUNK, h * HD : (h + 1) * HD]
        phase[u] = nn(jnp.concatenate([k] * 3, axis=1), f3)

    def feature(u):
        i, j, h = u
        c, s = wave(phase.pop(u), 1 / math.sqrt(half))
        feats[u] = jnp.concatenate([c.astype(BF), s.astype(BF)], axis=1)
        kf_ref[i * size + j : i * size + j + CHUNK, h * feat : (h + 1) * feat] = feats[u]

    def gather(u):
        i, j, h = u
        mine = slice(h * HD, (h + 1) * HD)
        sc_ref[(i * size + j) // CHUNK, mine, :] = state[h].astype(BF)
        state[h] = state[h] + nn(val[i][mine, j : j + CHUNK], feats.pop(u))

    project(0)
    for t in range(len(units) + 2):
        if t % per == per // 2 and t // per + 1 < count:
            project(t // per + 1)
        if t < len(units):
            turn(units[t])
        if 0 <= t - 1 < len(units):
            feature(units[t - 1])
        if 0 <= t - 2 < len(units):
            gather(units[t - 2])
    for h in range(heads):
        tot_ref[h * HD : (h + 1) * HD, :] = state[h].astype(BF)
    own_ref[...] = jnp.concatenate([pick_ref[c] for c in range(pick_ref.shape[0])], axis=1)


def key_pass(tokens, wkt, wvt, freq, picks, size):
    total, d = tokens.shape
    wid = wkt.shape[0]
    feat = 2 * freq.shape[1]
    heads = wid // HD
    return pl.pallas_call(
        functools.partial(key_kernel, size),
        in_specs=[FAR] * 5,
        out_specs=[HERE] * 6,
        out_shape=[
            jax.ShapeDtypeStruct(tokens.shape, BF),
            jax.ShapeDtypeStruct((total, heads * feat), BF),
            jax.ShapeDtypeStruct((wid, total), BF),
            jax.ShapeDtypeStruct((total // CHUNK, wid, feat), BF),
            jax.ShapeDtypeStruct((wid, feat), BF),
            jax.ShapeDtypeStruct((1, picks.size), jnp.int32),
        ],
        scratch_shapes=[
            pltpu.VMEM((2 * wid, d), BF),
            pltpu.VMEM(freq.shape, F32),
            pltpu.VMEM(picks.shape, jnp.int32),
            pltpu.SemaphoreType.DMA((4 + total // size,)),
        ],
        compiler_params=params(KEPT),
        cost_estimate=cost(5e9, 12e6),
        name="key_pass",
    )(*map(far, (tokens, wkt, wvt, freq, picks)))


def chosen(slot, pick_refs):
    row = pick_refs[0][...]
    for k in range(1, len(pick_refs)):
        row = jnp.where(slot == k, pick_refs[k][...], row)
    return row


def marks(row, rows):
    at = lax.broadcasted_iota(jnp.int32, (rows, row.shape[1]), 0)
    return (at == row).astype(F32).astype(BF)


def query_kernel(chunks, slots, picked, tok_ref, freq_ref, wqt_ref, kf_ref, vt_ref, sc_ref, *rest):
    pick_refs = rest[:picked]
    qft_ref, raw_ref = rest[-2 - (picked > 0) :][:2]
    wid = wqt_ref.shape[0]
    heads = wid // HD
    half = freq_ref.shape[1]
    feat = 2 * half
    rows = tok_ref.shape[0] // slots
    me = lax.axis_index("head")
    f3t = jnp.concatenate(parts(freq_ref[...].T * F32(0.5 / math.pi)), axis=1)
    place = [lax.broadcasted_iota(jnp.int32, (CHUNK, CHUNK), i) for i in (0, 1)]
    keep = place[0] <= place[1]
    units = [(c * CHUNK // rows, c * CHUNK % rows, h) for c in chunks for h in range(heads)]
    base = chunks[0] * CHUNK
    span = slice(base, base + len(chunks) * CHUNK)
    query = nt(tok_ref[span, :], wqt_ref[...]).astype(BF).T
    phase, feats, both = {}, {}, {}

    def spot(u):
        b, j, h = u
        return slice(h * HD, (h + 1) * HD), slice(b * rows + j, b * rows + j + CHUNK), slice(h * feat, (h + 1) * feat)

    def select(b):
        span = slice(b * rows, (b + 1) * rows)
        start = me * wid
        wide = -(-wid // LANES) * LANES
        low = pl.multiple_of(start // LANES * LANES, LANES)
        window = tok_ref[span, pl.ds(low, wide)]
        columns = window[:, :wid]
        for shift in range(math.gcd(wid, LANES), wide - wid + 1, math.gcd(wid, LANES)):
            columns = jnp.where(start % LANES == shift, window[:, shift : shift + wid], columns)
        rest[-1][b] = tn(columns, marks(chosen(me ^ b, pick_refs), rows)).astype(BF)

    def turn(u):
        mine, cols, _ = spot(u)
        q = query[mine, cols.start - base : cols.stop - base]
        phase[u] = nn(f3t, jnp.concatenate([q] * 3, axis=0))

    def feature(u):
        b, j, h = u
        c, s = wave(phase.pop(u), 1 / math.sqrt(half))
        feats[u] = jnp.concatenate([c.astype(BF), s.astype(BF)], axis=0)
        qft_ref[b, h * feat : (h + 1) * feat, j : j + CHUNK] = feats[u]

    def score(u):
        mine, cols, lines = spot(u)
        keys = jnp.concatenate([kf_ref[cols, lines], sc_ref[cols.start // CHUNK, mine, :]], axis=0)
        both[u] = nn(keys, feats.pop(u))

    def total(u):
        b, j, h = u
        mine, cols, _ = spot(u)
        got = both.pop(u)
        scores = jnp.where(keep, got[:CHUNK], 0.0).astype(BF)
        raw_ref[b, mine, j : j + CHUNK] = nn(vt_ref[mine, cols], scores) + got[CHUNK:]

    stages = (turn, feature, score, total)
    lag = 2
    for t in range(len(units) + lag * (len(stages) - 1)):
        if picked and t % heads == heads - 1 and t // heads < slots:
            select(t // heads)
        for i, stage in enumerate(stages):
            if 0 <= t - lag * i < len(units):
                stage(units[t - lag * i])


def query_pass(chunks, tokens, freq, wqt, kf, vt, sc, picks, slots, into):
    total, d = tokens.shape
    rows = total // slots
    wid = wqt.shape[0]
    feat = 2 * freq.shape[1]
    heads = wid // HD
    out_shape = [
        jax.ShapeDtypeStruct((slots, heads * feat, rows), BF),
        jax.ShapeDtypeStruct((slots, wid, rows), F32),
    ]
    if picks:
        out_shape.append(jax.ShapeDtypeStruct((slots, wid, picks[0].shape[1]), BF))
    args = [tokens, freq, wqt, kf, vt, sc, *picks, *into]
    return pl.pallas_call(
        functools.partial(query_kernel, chunks, slots, len(picks)),
        in_specs=[HERE] * (len(args) - len(into)) + [AWAY] * len(into),
        out_specs=[HERE] * len(out_shape),
        out_shape=out_shape,
        input_output_aliases={len(args) - len(into) + i: i for i in range(2) if into},
        compiler_params=params(KEPT),
        cost_estimate=cost(5e8 * len(chunks), 1e6 * len(chunks)),
        name="query_pass",
    )(*args)


def norm_kernel(slots, cap, rounds, raw_ref, qft_ref, seen_ref, *rest):
    got_refs, pick_refs = rest[:rounds], rest[rounds : rounds + slots]
    outs = rest[rounds + slots : rounds + slots + 3]
    sent_hbm, ready, acc, sent, sems = rest[rounds + slots + 3 :]
    me, at = lax.axis_index("head"), lax.axis_index("seq")
    wid = raw_ref.shape[1]
    heads = wid // HD
    feat = got_refs[0].shape[1]
    before = jnp.zeros(got_refs[0].shape, F32)
    for i, got in enumerate(got_refs):
        before = before + jnp.where((at & (1 << i)) > 0, got[...].astype(F32), 0.0)
    before = before.astype(BF)
    goals = [outs[0], outs[1].at[pl.ds(0, wid)], outs[2], outs[1].at[pl.ds(wid, wid)]]
    copies = [pltpu.make_async_copy(ready.at[k], goals[k], sems.at[k]) for k in range(slots)]
    picked = {}

    def norm(k):
        block = me ^ k
        for h in range(heads):
            mine = slice(h * HD, (h + 1) * HD)
            raw = raw_ref[block, mine, :] + nn(before[mine, :], qft_ref[block, h * feat : (h + 1) * feat, :])
            meansq = jnp.mean(raw * raw, axis=0, keepdims=True)
            ready[k, mine, :] = (raw * lax.rsqrt(meansq + F32(EPS))).astype(BF)
        copies[k].start()

    def pick(k):
        picked[k] = nn(ready[k], marks(pick_refs[k][...], ready.shape[2])).astype(BF)

    def spread(k):
        both = jnp.concatenate([picked.pop(k), seen_ref[me ^ k]], axis=0)
        n = both.shape[1]
        experts = n // cap
        entry = lax.broadcasted_iota(jnp.int32, (1, n), 1)
        row = (entry % experts * slots + (me ^ k)) * cap + entry // experts
        part = nt(marks(row, acc.shape[0]), both)
        acc[...] = part if k == 0 else acc[...] + part

    stages = (norm, pick, spread)
    for t in range(slots + len(stages) - 1):
        for i, stage in enumerate(stages):
            if 0 <= t - i < slots:
                stage(t - i)
    sent[...] = acc[...].astype(BF)
    last = pltpu.make_async_copy(sent, sent_hbm, sems.at[slots])
    last.start()
    for copy in copies:
        copy.wait()
    last.wait()


def norm_pass(raw, qft, seen, got, picks, cap):
    slots, wid, rows = raw.shape
    n = slots * picks[0].shape[1]
    return pl.pallas_call(
        functools.partial(norm_kernel, slots, cap, len(got)),
        in_specs=[HERE] * (3 + len(got) + slots),
        out_specs=[FAR] * 4,
        out_shape=[pltpu.HBM(x, BF) for x in ((wid, rows), (2 * wid, rows), (wid, rows), (n, 2 * wid))],
        scratch_shapes=[
            pltpu.VMEM((slots, wid, rows), BF),
            pltpu.VMEM((n, 2 * wid), F32),
            pltpu.VMEM((n, 2 * wid), BF),
            pltpu.SemaphoreType.DMA((slots + 1,)),
        ],
        compiler_params=params(KEPT + n * wid * 20 // MIB),
        cost_estimate=cost(3e9, 8e6),
        name="norm_pass",
    )(raw, qft, seen, *got, *picks)


def expert_kernel(cap, ups, downs, got_hbm, wo_hbm, wi_hbm, wd_hbm, out_ref, got, wo, wi, wd, taken, acc, sems):
    slots, ring, each, both = got.shape
    wid = both // 2
    n, d = ring * each, wo.shape[2]
    ff = wi.shape[1]
    landing = [pltpu.make_async_copy(got_hbm.at[:, h], got.at[h], sems.at[h]) for h in range(slots)]
    landing.append(pltpu.make_async_copy(wo_hbm, wo, sems.at[slots]))
    up = ff // ups
    rise = []
    for t in range(ups):
        cut = pl.ds(t * up, up)
        rise.append(pltpu.make_async_copy(wi_hbm.at[0, :, cut], wi.at[:, cut], sems.at[slots + 1 + t]))
    down = ff // downs
    fall = []
    for t in range(downs):
        cut = pl.ds(t * down, down)
        fall.append(pltpu.make_async_copy(wd_hbm.at[0, cut, :], wd.at[cut, :], sems.at[slots + 1 + ups + t]))
    for c in landing + rise + fall:
        c.start()
    for c in landing:
        c.wait()
    parts_in = [got[h].reshape(n, both) for h in range(slots)]
    mixed = jnp.concatenate([g.astype(F32)[:, wid:] for g in parts_in], axis=1)
    for h, g in enumerate(parts_in):
        mixed = mixed + nn(g[:, :wid], wo[h])
    taken[...] = mixed.astype(BF)
    inner = []
    for t in range(ups):
        rise[t].wait()
        part = nn(taken[...], wi[:, t * up : (t + 1) * up])
        inner.append(jax.nn.gelu(part, approximate=True).astype(BF))
    inner = jnp.concatenate(inner, axis=1)
    for t in range(downs):
        fall[t].wait()
        part = nn(inner[:, t * down : (t + 1) * down], wd[t * down : (t + 1) * down, :])
        acc[...] = part if t == 0 else acc[...] + part
    m = out_ref.shape[0]
    at = lax.broadcasted_iota(jnp.int32, (1, n), 1)
    out_ref[...] = nn(marks(at // cap * PAD + at % cap, m), acc[...].astype(BF)).astype(BF)


def expert_pass(arrived, w_out, w_in, w_down, cap, ups=3, downs=3):
    ring, slots, each, both = arrived.shape
    d, ff = w_in.shape[1:]
    m = ring * each // cap * PAD
    return pl.pallas_call(
        functools.partial(expert_kernel, cap, ups, downs),
        in_specs=[AWAY] + [FAR] * 3,
        out_specs=HERE,
        out_shape=jax.ShapeDtypeStruct((m, d), BF),
        scratch_shapes=[
            pltpu.VMEM((slots, ring, each, both), BF),
            pltpu.VMEM(w_out.shape, BF),
            pltpu.VMEM((d, ff), BF),
            pltpu.VMEM((ff, d), BF),
            pltpu.VMEM((ring * each, d), BF),
            pltpu.VMEM((ring * each, d), F32),
            pltpu.SemaphoreType.DMA((slots + 1 + ups + downs,)),
        ],
        compiler_params=params(40),
        cost_estimate=cost(2e9, 12e6),
        name="expert_pass",
    )(arrived, *map(far, (w_out, w_in, w_down)))


def hidden_kernel(tok_hbm, wo_hbm, own_hbm, near_hbm, far_hbm, router_ref, pick_ref, *rest):
    hid_ref, comb_ref, tok, wo, attn, sems = rest
    me = lax.axis_index("head")
    rows = tok.shape[0]
    group, wid = wo_hbm.shape[:2]
    first = pl.multiple_of(me * rows, rows)
    pieces = [own_hbm, near_hbm.at[pl.ds(0, wid)], far_hbm.at[pl.ds(0, wid)], far_hbm.at[pl.ds(wid, wid)]]
    copies = [pltpu.make_async_copy(tok_hbm.at[pl.ds(first, rows)], tok, sems.at[0])]
    for k in range(group):
        line = pl.ds(k * wid, wid)
        copies.append(pltpu.make_async_copy(wo_hbm.at[me ^ k], wo.at[line], sems.at[1 + k]))
        copies.append(pltpu.make_async_copy(pieces[k], attn.at[line], sems.at[1 + group + k]))
    for copy in copies:
        copy.start()
    for copy in copies:
        copy.wait()
    experts, n = router_ref.shape[0], pick_ref.shape[1]
    spreads = marks(lax.broadcasted_iota(jnp.int32, (1, n), 1) // PAD, experts)
    hidden = (tok[...].astype(F32) + tn(attn[...], wo[...])).astype(BF)
    hid_ref[...] = hidden
    gate = jax.nn.sigmoid(nt(hidden, router_ref[...])).astype(BF)
    at = lax.broadcasted_iota(jnp.int32, (rows, n), 0)
    comb_ref[...] = jnp.where(pick_ref[...] == at, nn(gate, spreads), 0.0).astype(BF)


def hidden_pass(tokens, w_out, own, near, across, router_t, pick_row):
    d = tokens.shape[1]
    group, wid = w_out.shape[:2]
    rows = tokens.shape[0] // group
    n = pick_row.shape[1]
    return pl.pallas_call(
        hidden_kernel,
        in_specs=[FAR] * 2 + [AWAY] * 3 + [HERE] * 2,
        out_specs=[HERE] * 2,
        out_shape=[jax.ShapeDtypeStruct((rows, d), BF), jax.ShapeDtypeStruct((rows, n), BF)],
        scratch_shapes=[
            pltpu.VMEM((rows, d), BF),
            pltpu.VMEM((group * wid, d), BF),
            pltpu.VMEM((group * wid, rows), BF),
            pltpu.SemaphoreType.DMA((1 + 2 * group,)),
        ],
        compiler_params=params(),
        cost_estimate=cost(2e9, 6e6),
        name="hidden_pass",
    )(far(tokens), far(w_out), own, near, across, router_t, pick_row)


def combine_kernel(tiles, hid_hbm, comb_hbm, back_hbm, out_hbm, hid, comb, back, out, in_sems, out_sems):
    rows = hid.shape[0]
    tile = rows // tiles
    cuts = [pl.ds(t * tile, tile) for t in range(tiles)]
    need = pltpu.make_async_copy(back_hbm, back, in_sems.at[0])
    loads = [
        [
            pltpu.make_async_copy(comb_hbm.at[c], comb.at[c], in_sems.at[1 + 2 * t]),
            pltpu.make_async_copy(hid_hbm.at[c], hid.at[c], in_sems.at[2 + 2 * t]),
        ]
        for t, c in enumerate(cuts)
    ]
    stores = [pltpu.make_async_copy(out.at[c], out_hbm.at[c], out_sems.at[t]) for t, c in enumerate(cuts)]
    need.start()
    for pair in loads:
        for copy in pair:
            copy.start()
    need.wait()
    for t, cut in enumerate(cuts):
        for copy in loads[t]:
            copy.wait()
        out[cut, :] = (hid[cut, :].astype(F32) + nn(comb[cut, :], back[...])).astype(BF)
        stores[t].start()
    for store in stores:
        store.wait()


def combine_pass(hidden, comb, back, tiles=2):
    rows, d = hidden.shape
    return pl.pallas_call(
        functools.partial(combine_kernel, tiles),
        in_specs=[FAR, FAR, AWAY],
        out_specs=AWAY,
        out_shape=jax.ShapeDtypeStruct((rows, d), BF),
        scratch_shapes=[
            pltpu.VMEM(hidden.shape, BF),
            pltpu.VMEM(comb.shape, BF),
            pltpu.VMEM(back.shape, BF),
            pltpu.VMEM(hidden.shape, BF),
            pltpu.SemaphoreType.DMA((1 + 2 * tiles,)),
            pltpu.SemaphoreType.DMA((tiles,)),
        ],
        compiler_params=params(40),
        cost_estimate=cost(1e9, 4e6),
        name="combine_pass",
    )(far(hidden), far(comb), back)


def per_device(tokens, w_query, w_key, w_value, freq, w_out, router, w_in, w_down, picks):
    total, d = tokens.shape
    group = lax.axis_size("head")
    ring = lax.axis_size("seq")
    rows = total // group
    experts, _, cap = picks.shape
    wid = w_query.shape[1]

    pick_row = jnp.pad(picks[:, 0, :], ((0, 0), (0, PAD - cap)), constant_values=-1).reshape(1, experts * PAD)
    swap = lambda x, k: lax.ppermute(x, "head", [(i, i ^ k) for i in range(group)])

    tok_here, kf, vt, sc, held, own = key_pass(
        tokens, w_key.T, w_value.T, freq, picks.transpose(2, 1, 0), rows
    )
    near = [own] + [swap(own, k) for k in range(1, group)]
    got, made = [], []
    chunks = total // CHUNK
    rounds = ring.bit_length() - 1
    for i in range(rounds):
        got.append(lax.ppermute(held, "seq", [(j, j ^ (1 << i)) for j in range(ring)]))
        part = range(chunks * i // rounds, chunks * (i + 1) // rounds)
        made = query_pass(
            part, tok_here, freq, w_query.T, kf, vt, sc, near if i == rounds - 1 else [], group, made
        )
        both = held.astype(F32) + got[-1].astype(F32)
        held, *made = lax.optimization_barrier([both.astype(BF), *made])
    qft, raw, seen = made
    mine, near_out, across, sent = norm_pass(raw, qft, seen, got, near, cap)

    sent = sent.reshape(experts, group * cap, 2 * wid)
    arrived = lax.all_to_all(sent, ("seq", "head"), split_axis=0, concat_axis=0, tiled=True)
    near_got = swap(near_out, 1)
    across = swap(jnp.concatenate([across, near_got[wid:]]), 2)
    arrived, pick_row = lax.optimization_barrier((arrived, pick_row))
    w_out = w_out.reshape(group, wid, d)
    result = expert_pass(
        arrived.reshape(ring, group, group * cap, 2 * wid), w_out, w_in, w_down, cap
    )
    back = lax.all_to_all(
        result.reshape(experts, PAD, d), ("seq", "head"), split_axis=0, concat_axis=0, tiled=True
    )
    hidden, comb = hidden_pass(tokens, w_out, mine, near_got, across, router.T, pick_row)
    return combine_pass(hidden, comb, back.reshape(experts * PAD, d))


def solution(mesh):
    in_specs = (
        P("seq", None),
        P(None, "head"),
        P(None, "head"),
        P(None, "head"),
        P(),
        P(),
        P(),
        P(("seq", "head"), None, None),
        P(("seq", "head"), None, None),
        P(None, ("seq", "head"), None),
    )
    out_specs = P(("seq", "head"), None)
    return jax.shard_map(
        per_device, mesh=mesh, in_specs=in_specs, out_specs=out_specs, check_vma=False
    )
```

```python
import functools
import math

import jax
import jax.numpy as jnp
from jax import lax
from jax.experimental import pallas as pl
from jax.experimental.pallas import tpu as pltpu
from jax.sharding import PartitionSpec as P

HD = 64
EPS = 1e-06
CHUNK = 256
PAD = 8
BF = jnp.bfloat16
F32 = jnp.float32
MIB = 2**20
KEPT = 24
LANES = 128
SIN = (3.14158202, -5.16714279, 2.54189901, -0.55463616)
COS = (0.9999933, -4.93393802, 4.04128381, -1.22212701)


def nn(a, b):
    return lax.dot_general(a, b, (((1,), (0,)), ((), ())), preferred_element_type=F32)


def nt(a, b):
    return lax.dot_general(a, b, (((1,), (1,)), ((), ())), preferred_element_type=F32)


def tn(a, b):
    return lax.dot_general(a, b, (((0,), (0,)), ((), ())), preferred_element_type=F32)


def wave(turns, scale):
    big = F32(1.5 * 2.0**23)
    r = turns - ((turns + big) - big)
    u = r * r
    root = math.sqrt(2 * scale)
    a = [F32(v * root) for v in SIN]
    b = [F32(v * root) for v in COS]
    s = r * (a[0] + u * (a[1] + u * (a[2] + u * a[3])))
    c = b[0] + u * (b[1] + u * (b[2] + u * b[3]))
    return F32(scale) - s * s, s * c


def parts(f):
    hi = f.astype(BF)
    rest = f - hi.astype(F32)
    mid = rest.astype(BF)
    lo = (rest - mid.astype(F32)).astype(BF)
    return [hi, mid, lo]


def whole(shape):
    return pl.BlockSpec(shape, lambda *_: (0,) * len(shape))


def params(mib=60):
    return pltpu.CompilerParams(vmem_limit_bytes=mib * MIB)


def far(x):
    return pltpu.with_memory_space_constraint(x, pltpu.HBM)


def cost(flops, nbytes):
    return pl.CostEstimate(flops=int(flops), bytes_accessed=int(nbytes), transcendentals=0)


HERE = pl.BlockSpec(memory_space=pltpu.VMEM)
AWAY = pl.BlockSpec(memory_space=pl.ANY)
FAR = pl.BlockSpec(memory_space=pltpu.HBM)


def key_kernel(size, tok_hbm, wkt_hbm, wvt_hbm, freq_hbm, pick_hbm, *rest):
    tok_ref, kf_ref, vt_ref, sc_ref, tot_ref, own_ref, w_ref, freq_ref, pick_ref, sems = rest
    total = tok_ref.shape[0]
    wid = wkt_hbm.shape[0]
    heads = wid // HD
    half = freq_ref.shape[1]
    feat = 2 * half
    count = total // size
    weights = [
        pltpu.make_async_copy(w, w_ref.at[pl.ds(i * wid, wid)], sems.at[i])
        for i, w in enumerate((wkt_hbm, wvt_hbm))
    ]
    weights.append(pltpu.make_async_copy(freq_hbm, freq_ref, sems.at[2]))
    weights.append(pltpu.make_async_copy(pick_hbm, pick_ref, sems.at[3]))
    loads = [
        pltpu.make_async_copy(
            tok_hbm.at[pl.ds(i * size, size)], tok_ref.at[pl.ds(i * size, size)], sems.at[4 + i]
        )
        for i in range(count)
    ]
    for copy in [weights[0], loads[0], *weights[1:], *loads[1:]]:
        copy.start()
    for copy in weights:
        copy.wait()
    f3 = jnp.concatenate(parts(freq_ref[...] * F32(0.5 / math.pi)), axis=0)
    state = [jnp.zeros((HD, feat), F32) for _ in range(heads)]
    units = [(i, j, h) for i in range(count) for j in range(0, size, CHUNK) for h in range(heads)]
    per = len(units) // count
    key, val, phase, feats = {}, {}, {}, {}

    def project(i):
        loads[i].wait()
        span = slice(i * size, (i + 1) * size)
        out = nt(tok_ref[span, :], w_ref[...]).astype(BF)
        key[i] = out[:, :wid]
        val[i] = out[:, wid:].T
        vt_ref[:, span] = val[i]

    def turn(u):
        i, j, h = u
        k = key[i][j : j + CHUNK, h * HD : (h + 1) * HD]
        phase[u] = nn(jnp.concatenate([k] * 3, axis=1), f3)

    def feature(u):
        i, j, h = u
        c, s = wave(phase.pop(u), 1 / math.sqrt(half))
        feats[u] = jnp.concatenate([c.astype(BF), s.astype(BF)], axis=1)
        kf_ref[i * size + j : i * size + j + CHUNK, h * feat : (h + 1) * feat] = feats[u]

    def gather(u):
        i, j, h = u
        mine = slice(h * HD, (h + 1) * HD)
        sc_ref[(i * size + j) // CHUNK, mine, :] = state[h].astype(BF)
        state[h] = state[h] + nn(val[i][mine, j : j + CHUNK], feats.pop(u))

    project(0)
    for t in range(len(units) + 2):
        if t % per == per // 2 and t // per + 1 < count:
            project(t // per + 1)
        if t < len(units):
            turn(units[t])
        if 0 <= t - 1 < len(units):
            feature(units[t - 1])
        if 0 <= t - 2 < len(units):
            gather(units[t - 2])
    for h in range(heads):
        tot_ref[h * HD : (h + 1) * HD, :] = state[h].astype(BF)
    own_ref[...] = jnp.concatenate([pick_ref[c] for c in range(pick_ref.shape[0])], axis=1)


def key_pass(tokens, wkt, wvt, freq, picks, size):
    total, d = tokens.shape
    wid = wkt.shape[0]
    feat = 2 * freq.shape[1]
    heads = wid // HD
    return pl.pallas_call(
        functools.partial(key_kernel, size),
        in_specs=[FAR] * 5,
        out_specs=[HERE] * 6,
        out_shape=[
            jax.ShapeDtypeStruct(tokens.shape, BF),
            jax.ShapeDtypeStruct((total, heads * feat), BF),
            jax.ShapeDtypeStruct((wid, total), BF),
            jax.ShapeDtypeStruct((total // CHUNK, wid, feat), BF),
            jax.ShapeDtypeStruct((wid, feat), BF),
            jax.ShapeDtypeStruct((1, picks.size), jnp.int32),
        ],
        scratch_shapes=[
            pltpu.VMEM((2 * wid, d), BF),
            pltpu.VMEM(freq.shape, F32),
            pltpu.VMEM(picks.shape, jnp.int32),
            pltpu.SemaphoreType.DMA((4 + total // size,)),
        ],
        compiler_params=params(KEPT),
        cost_estimate=cost(5e9, 12e6),
        name="key_pass",
    )(*map(far, (tokens, wkt, wvt, freq, picks)))


def chosen(slot, pick_refs):
    row = pick_refs[0][...]
    for k in range(1, len(pick_refs)):
        row = jnp.where(slot == k, pick_refs[k][...], row)
    return row


def marks(row, rows):
    at = lax.broadcasted_iota(jnp.int32, (rows, row.shape[1]), 0)
    return (at == row).astype(F32).astype(BF)


def query_kernel(chunks, slots, picked, tok_ref, freq_ref, wqt_ref, kf_ref, vt_ref, sc_ref, *rest):
    pick_refs = rest[:picked]
    qft_ref, raw_ref = rest[-2 - (picked > 0) :][:2]
    wid = wqt_ref.shape[0]
    heads = wid // HD
    half = freq_ref.shape[1]
    feat = 2 * half
    rows = tok_ref.shape[0] // slots
    me = lax.axis_index("head")
    f3t = jnp.concatenate(parts(freq_ref[...].T * F32(0.5 / math.pi)), axis=1)
    place = [lax.broadcasted_iota(jnp.int32, (CHUNK, CHUNK), i) for i in (0, 1)]
    keep = place[0] <= place[1]
    units = [(c * CHUNK // rows, c * CHUNK % rows, h) for c in chunks for h in range(heads)]
    base = chunks[0] * CHUNK
    span = slice(base, base + len(chunks) * CHUNK)
    query = nt(tok_ref[span, :], wqt_ref[...]).astype(BF).T
    phase, feats, both = {}, {}, {}

    def spot(u):
        b, j, h = u
        return slice(h * HD, (h + 1) * HD), slice(b * rows + j, b * rows + j + CHUNK), slice(h * feat, (h + 1) * feat)

    def select(b):
        span = slice(b * rows, (b + 1) * rows)
        start = me * wid
        wide = -(-wid // LANES) * LANES
        low = pl.multiple_of(start // LANES * LANES, LANES)
        window = tok_ref[span, pl.ds(low, wide)]
        columns = window[:, :wid]
        for shift in range(math.gcd(wid, LANES), wide - wid + 1, math.gcd(wid, LANES)):
            columns = jnp.where(start % LANES == shift, window[:, shift : shift + wid], columns)
        line = chosen(me ^ b, pick_refs).T
        at = lax.broadcasted_iota(jnp.int32, (line.shape[0], rows), 1)
        rest[-1][b] = nn((at == line).astype(F32).astype(BF), columns).astype(BF).T

    def turn(u):
        mine, cols, _ = spot(u)
        q = query[mine, cols.start - base : cols.stop - base]
        phase[u] = nn(f3t, jnp.concatenate([q] * 3, axis=0))

    def feature(u):
        b, j, h = u
        c, s = wave(phase.pop(u), 1 / math.sqrt(half))
        feats[u] = jnp.concatenate([c.astype(BF), s.astype(BF)], axis=0)
        qft_ref[b, h * feat : (h + 1) * feat, j : j + CHUNK] = feats[u]

    def score(u):
        mine, cols, lines = spot(u)
        keys = jnp.concatenate([kf_ref[cols, lines], sc_ref[cols.start // CHUNK, mine, :]], axis=0)
        both[u] = nn(keys, feats.pop(u))

    def total(u):
        b, j, h = u
        mine, cols, _ = spot(u)
        got = both.pop(u)
        scores = jnp.where(keep, got[:CHUNK], 0.0).astype(BF)
        raw_ref[b, mine, j : j + CHUNK] = nn(vt_ref[mine, cols], scores) + got[CHUNK:]

    stages = (turn, feature, score, total)
    lag = 2
    for t in range(len(units) + lag * (len(stages) - 1)):
        if picked and t % heads == heads - 1 and t // heads < slots:
            select(t // heads)
        for i, stage in enumerate(stages):
            if 0 <= t - lag * i < len(units):
                stage(units[t - lag * i])


def query_pass(chunks, tokens, freq, wqt, kf, vt, sc, picks, slots, into):
    total, d = tokens.shape
    rows = total // slots
    wid = wqt.shape[0]
    feat = 2 * freq.shape[1]
    heads = wid // HD
    out_shape = [
        jax.ShapeDtypeStruct((slots, heads * feat, rows), BF),
        jax.ShapeDtypeStruct((slots, wid, rows), F32),
    ]
    if picks:
        out_shape.append(jax.ShapeDtypeStruct((slots, wid, picks[0].shape[1]), BF))
    args = [tokens, freq, wqt, kf, vt, sc, *picks, *into]
    return pl.pallas_call(
        functools.partial(query_kernel, chunks, slots, len(picks)),
        in_specs=[HERE] * (len(args) - len(into)) + [AWAY] * len(into),
        out_specs=[HERE] * len(out_shape),
        out_shape=out_shape,
        input_output_aliases={len(args) - len(into) + i: i for i in range(2) if into},
        compiler_params=params(KEPT),
        cost_estimate=cost(5e8 * len(chunks), 1e6 * len(chunks)),
        name="query_pass",
    )(*args)


def norm_kernel(slots, cap, rounds, raw_ref, qft_ref, seen_ref, *rest):
    got_refs, pick_refs = rest[:rounds], rest[rounds : rounds + slots]
    outs = rest[rounds + slots : rounds + slots + 3]
    sent_hbm, ready, acc, sent, sems = rest[rounds + slots + 3 :]
    me, at = lax.axis_index("head"), lax.axis_index("seq")
    wid = raw_ref.shape[1]
    heads = wid // HD
    feat = got_refs[0].shape[1]
    before = jnp.zeros(got_refs[0].shape, F32)
    for i, got in enumerate(got_refs):
        before = before + jnp.where((at & (1 << i)) > 0, got[...].astype(F32), 0.0)
    before = before.astype(BF)
    goals = [outs[0], outs[1].at[pl.ds(0, wid)], outs[2], outs[1].at[pl.ds(wid, wid)]]
    copies = [pltpu.make_async_copy(ready.at[k], goals[k], sems.at[k]) for k in range(slots)]
    picked = {}

    def norm(k):
        block = me ^ k
        for h in range(heads):
            mine = slice(h * HD, (h + 1) * HD)
            raw = raw_ref[block, mine, :] + nn(before[mine, :], qft_ref[block, h * feat : (h + 1) * feat, :])
            meansq = jnp.mean(raw * raw, axis=0, keepdims=True)
            ready[k, mine, :] = (raw * lax.rsqrt(meansq + F32(EPS))).astype(BF)
        copies[k].start()

    def pick(k):
        picked[k] = nn(ready[k], marks(pick_refs[k][...], ready.shape[2])).astype(BF)

    def spread(k):
        both = jnp.concatenate([picked.pop(k), seen_ref[me ^ k]], axis=0)
        n = both.shape[1]
        experts = n // cap
        entry = lax.broadcasted_iota(jnp.int32, (1, n), 1)
        row = (entry % experts * slots + (me ^ k)) * cap + entry // experts
        part = nt(marks(row, acc.shape[0]), both)
        acc[...] = part if k == 0 else acc[...] + part

    stages = (norm, pick, spread)
    for t in range(slots + len(stages) - 1):
        for i, stage in enumerate(stages):
            if 0 <= t - i < slots:
                stage(t - i)
    sent[...] = acc[...].astype(BF)
    last = pltpu.make_async_copy(sent, sent_hbm, sems.at[slots])
    last.start()
    for copy in copies:
        copy.wait()
    last.wait()


def norm_pass(raw, qft, seen, got, picks, cap):
    slots, wid, rows = raw.shape
    n = slots * picks[0].shape[1]
    return pl.pallas_call(
        functools.partial(norm_kernel, slots, cap, len(got)),
        in_specs=[HERE] * (3 + len(got) + slots),
        out_specs=[FAR] * 4,
        out_shape=[pltpu.HBM(x, BF) for x in ((wid, rows), (2 * wid, rows), (wid, rows), (n, 2 * wid))],
        scratch_shapes=[
            pltpu.VMEM((slots, wid, rows), BF),
            pltpu.VMEM((n, 2 * wid), F32),
            pltpu.VMEM((n, 2 * wid), BF),
            pltpu.SemaphoreType.DMA((slots + 1,)),
        ],
        compiler_params=params(KEPT + n * wid * 20 // MIB),
        cost_estimate=cost(3e9, 8e6),
        name="norm_pass",
    )(raw, qft, seen, *got, *picks)


def packing(d, cap):
    spare = PAD - cap
    columns = d // LANES
    tiles = -(-columns * cap // PAD)
    left = [(c, first) for c in range(tiles, columns) for first in range(0, cap, spare)]
    rest = [left[t : t + 1] for t in range(tiles)]
    return tiles, rest


def expert_kernel(cap, ups, downs, got_hbm, wo_hbm, wi_hbm, wd_hbm, out_ref, got, wo, wi, wd, taken, acc, sems):
    slots, ring, each, both = got.shape
    wid = both // 2
    n, d = ring * each, wo.shape[2]
    ff = wi.shape[1]
    landing = [pltpu.make_async_copy(got_hbm.at[:, h], got.at[h], sems.at[h]) for h in range(slots)]
    landing.append(pltpu.make_async_copy(wo_hbm, wo, sems.at[slots]))
    up = ff // ups
    rise = []
    for t in range(ups):
        cut = pl.ds(t * up, up)
        rise.append(pltpu.make_async_copy(wi_hbm.at[0, :, cut], wi.at[:, cut], sems.at[slots + 1 + t]))
    down = ff // downs
    fall = []
    for t in range(downs):
        cut = pl.ds(t * down, down)
        fall.append(pltpu.make_async_copy(wd_hbm.at[0, cut, :], wd.at[cut, :], sems.at[slots + 1 + ups + t]))
    for c in landing + rise + fall:
        c.start()
    for c in landing:
        c.wait()
    parts_in = [got[h].reshape(n, both) for h in range(slots)]
    mixed = jnp.concatenate([g.astype(F32)[:, wid:] for g in parts_in], axis=1)
    for h, g in enumerate(parts_in):
        mixed = mixed + nn(g[:, :wid], wo[h])
    taken[...] = mixed.astype(BF)
    inner = []
    for t in range(ups):
        rise[t].wait()
        part = nn(taken[...], wi[:, t * up : (t + 1) * up])
        inner.append(jax.nn.gelu(part, approximate=True).astype(BF))
    inner = jnp.concatenate(inner, axis=1)
    for t in range(downs):
        fall[t].wait()
        part = nn(inner[:, t * down : (t + 1) * down], wd[t * down : (t + 1) * down, :])
        acc[...] = part if t == 0 else acc[...] + part
    ready = acc[...].astype(BF)
    tiles, rest = packing(d, cap)
    blocks = n // cap
    line = lax.broadcasted_iota(jnp.int32, (blocks * PAD, n), 0)
    entry = lax.broadcasted_iota(jnp.int32, (blocks * PAD, n), 1)
    same = (line // PAD == entry // cap) & (line % PAD < cap)
    plain = (same & (line % PAD == entry % cap)).astype(F32).astype(BF)
    body = nn(plain, ready[:, : tiles * LANES])
    for t in range(tiles):
        tile = body[:, t * LANES : (t + 1) * LANES]
        for column, first in rest[t]:
            extra = (line // PAD == entry // cap) & (line % PAD >= cap) & (entry % cap == line % PAD - cap + first)
            tile = tile + nn(extra.astype(F32).astype(BF), ready[:, column * LANES : (column + 1) * LANES])
        out_ref[:, t * PAD : (t + 1) * PAD, :] = tile.reshape(blocks, PAD, LANES).astype(BF)


def expert_pass(arrived, w_out, w_in, w_down, cap, ups=3, downs=3):
    ring, slots, each, both = arrived.shape
    d, ff = w_in.shape[1:]
    blocks = ring * each // cap
    tiles = packing(d, cap)[0]
    return pl.pallas_call(
        functools.partial(expert_kernel, cap, ups, downs),
        in_specs=[AWAY] + [FAR] * 3,
        out_specs=HERE,
        out_shape=jax.ShapeDtypeStruct((blocks, tiles * PAD, LANES), BF),
        scratch_shapes=[
            pltpu.VMEM((slots, ring, each, both), BF),
            pltpu.VMEM(w_out.shape, BF),
            pltpu.VMEM((d, ff), BF),
            pltpu.VMEM((ff, d), BF),
            pltpu.VMEM((ring * each, d), BF),
            pltpu.VMEM((ring * each, d), F32),
            pltpu.SemaphoreType.DMA((slots + 1 + ups + downs,)),
        ],
        compiler_params=params(40),
        cost_estimate=cost(2e9, 12e6),
        name="expert_pass",
    )(arrived, *map(far, (w_out, w_in, w_down)))


def hidden_kernel(tok_hbm, wo_hbm, own_hbm, near_hbm, far_hbm, router_ref, pick_ref, *rest):
    hid_ref, comb_ref, tok, wo, attn, sems = rest
    me = lax.axis_index("head")
    rows = tok.shape[0]
    group, wid = wo_hbm.shape[:2]
    first = pl.multiple_of(me * rows, rows)
    pieces = [own_hbm, near_hbm.at[pl.ds(0, wid)], far_hbm.at[pl.ds(0, wid)], far_hbm.at[pl.ds(wid, wid)]]
    copies = [pltpu.make_async_copy(tok_hbm.at[pl.ds(first, rows)], tok, sems.at[0])]
    for k in range(group):
        line = pl.ds(k * wid, wid)
        copies.append(pltpu.make_async_copy(wo_hbm.at[me ^ k], wo.at[line], sems.at[1 + k]))
        copies.append(pltpu.make_async_copy(pieces[k], attn.at[line], sems.at[1 + group + k]))
    for copy in copies:
        copy.start()
    for copy in copies:
        copy.wait()
    experts, n = router_ref.shape[0], pick_ref.shape[1]
    spreads = marks(lax.broadcasted_iota(jnp.int32, (1, n), 1) // PAD, experts)
    hidden = (tok[...].astype(F32) + tn(attn[...], wo[...])).astype(BF)
    hid_ref[...] = hidden
    gate = jax.nn.sigmoid(nt(hidden, router_ref[...])).astype(BF)
    at = lax.broadcasted_iota(jnp.int32, (rows, n), 0)
    weight = nn(gate, spreads)
    for i in range(comb_ref.shape[0]):
        comb_ref[i] = jnp.where(pick_ref[i : i + 1, :] == at, weight, 0.0).astype(BF)


def hidden_pass(tokens, w_out, own, near, across, router_t, pick_row):
    d = tokens.shape[1]
    group, wid = w_out.shape[:2]
    rows = tokens.shape[0] // group
    kinds, n = pick_row.shape
    return pl.pallas_call(
        hidden_kernel,
        in_specs=[FAR] * 2 + [AWAY] * 3 + [HERE] * 2,
        out_specs=[HERE] * 2,
        out_shape=[jax.ShapeDtypeStruct((rows, d), BF), jax.ShapeDtypeStruct((kinds, rows, n), BF)],
        scratch_shapes=[
            pltpu.VMEM((rows, d), BF),
            pltpu.VMEM((group * wid, d), BF),
            pltpu.VMEM((group * wid, rows), BF),
            pltpu.SemaphoreType.DMA((1 + 2 * group,)),
        ],
        compiler_params=params(),
        cost_estimate=cost(2e9, 6e6),
        name="hidden_pass",
    )(far(tokens), far(w_out), own, near, across, router_t, pick_row)


def combine_kernel(tiles, cap, hid_hbm, comb_hbm, back_hbm, out_hbm, hid, comb, back, out, in_sems, out_sems):
    rows = hid.shape[0]
    tile = rows // tiles
    cuts = [pl.ds(t * tile, tile) for t in range(tiles)]
    need = pltpu.make_async_copy(back_hbm, back, in_sems.at[0])
    loads = [
        [
            pltpu.make_async_copy(comb_hbm.at[:, c], comb.at[:, c], in_sems.at[1 + 2 * t]),
            pltpu.make_async_copy(hid_hbm.at[c], hid.at[c], in_sems.at[2 + 2 * t]),
        ]
        for t, c in enumerate(cuts)
    ]
    stores = [pltpu.make_async_copy(out.at[c], out_hbm.at[c], out_sems.at[t]) for t, c in enumerate(cuts)]
    need.start()
    for pair in loads:
        for copy in pair:
            copy.start()
    packs, rest = packing(hid.shape[1], cap)
    left = {}
    for j, held in enumerate(rest):
        for column, first in held:
            left.setdefault(column, []).append((j, first))
    need.wait()
    got = [back[:, j * PAD : (j + 1) * PAD, :].reshape(comb.shape[2], LANES) for j in range(packs)]
    for t, cut in enumerate(cuts):
        for copy in loads[t]:
            copy.wait()
        for j in range(packs):
            lanes = slice(j * LANES, (j + 1) * LANES)
            out[cut, lanes] = (hid[cut, lanes].astype(F32) + nn(comb[0, cut, :], got[j])).astype(BF)
        for column, places in left.items():
            lanes = slice(column * LANES, (column + 1) * LANES)
            moe = sum(nn(comb[1 + first // (PAD - cap), cut, :], got[j]) for j, first in places)
            out[cut, lanes] = (hid[cut, lanes].astype(F32) + moe).astype(BF)
        stores[t].start()
    for store in stores:
        store.wait()


def combine_pass(hidden, comb, back, cap, tiles=3):
    rows, d = hidden.shape
    return pl.pallas_call(
        functools.partial(combine_kernel, tiles, cap),
        in_specs=[FAR, FAR, AWAY],
        out_specs=AWAY,
        out_shape=jax.ShapeDtypeStruct((rows, d), BF),
        scratch_shapes=[
            pltpu.VMEM(hidden.shape, BF),
            pltpu.VMEM(comb.shape, BF),
            pltpu.VMEM(back.shape, BF),
            pltpu.VMEM(hidden.shape, BF),
            pltpu.SemaphoreType.DMA((1 + 2 * tiles,)),
            pltpu.SemaphoreType.DMA((tiles,)),
        ],
        compiler_params=params(40),
        cost_estimate=cost(1e9, 4e6),
        name="combine_pass",
    )(far(hidden), far(comb), back)


def per_device(tokens, w_query, w_key, w_value, freq, w_out, router, w_in, w_down, picks):
    total, d = tokens.shape
    group = lax.axis_size("head")
    ring = lax.axis_size("seq")
    rows = total // group
    experts, _, cap = picks.shape
    wid = w_query.shape[1]

    spare = PAD - cap
    own_picks = picks[:, 0, :]
    kinds = [jnp.pad(own_picks, ((0, 0), (0, spare)), constant_values=-1)]
    for first in range(0, cap, spare):
        kinds.append(jnp.pad(own_picks[:, first : first + spare], ((0, 0), (cap, 0)), constant_values=-1))
    pick_row = jnp.stack(kinds).reshape(len(kinds), experts * PAD)
    swap = lambda x, k: lax.ppermute(x, "head", [(i, i ^ k) for i in range(group)])

    tok_here, kf, vt, sc, held, own = key_pass(
        tokens, w_key.T, w_value.T, freq, picks.transpose(2, 1, 0), rows
    )
    near = [own] + [swap(own, k) for k in range(1, group)]
    got, made = [], []
    chunks = total // CHUNK
    rounds = ring.bit_length() - 1
    for i in range(rounds):
        got.append(lax.ppermute(held, "seq", [(j, j ^ (1 << i)) for j in range(ring)]))
        part = range(chunks * i // rounds, chunks * (i + 1) // rounds)
        made = query_pass(
            part, tok_here, freq, w_query.T, kf, vt, sc, near if i == rounds - 1 else [], group, made
        )
        both = held.astype(F32) + got[-1].astype(F32)
        held, *made = lax.optimization_barrier([both.astype(BF), *made])
    qft, raw, seen = made
    mine, near_out, across, sent = norm_pass(raw, qft, seen, got, near, cap)

    sent = sent.reshape(experts, group * cap, 2 * wid)
    arrived = lax.all_to_all(sent, ("seq", "head"), split_axis=0, concat_axis=0, tiled=True)
    near_got = swap(near_out, 1)
    across = swap(jnp.concatenate([across, near_got[wid:]]), 2)
    arrived, pick_row = lax.optimization_barrier((arrived, pick_row))
    w_out = w_out.reshape(group, wid, d)
    result = expert_pass(
        arrived.reshape(ring, group, group * cap, 2 * wid), w_out, w_in, w_down, cap
    )
    back = lax.all_to_all(result, ("seq", "head"), split_axis=0, concat_axis=0, tiled=True)
    hidden, comb = hidden_pass(tokens, w_out, mine, near_got, across, router.T, pick_row)
    return combine_pass(hidden, comb, back, cap)


def solution(mesh):
    in_specs = (
        P("seq", None),
        P(None, "head"),
        P(None, "head"),
        P(None, "head"),
        P(),
        P(),
        P(),
        P(("seq", "head"), None, None),
        P(("seq", "head"), None, None),
        P(None, ("seq", "head"), None),
    )
    out_specs = P(("seq", "head"), None)
    return jax.shard_map(
        per_device, mesh=mesh, in_specs=in_specs, out_specs=out_specs, check_vma=False
    )
```

```python
import functools
import math

import jax
import jax.numpy as jnp
from jax import lax
from jax.experimental import pallas as pl
from jax.experimental.pallas import tpu as pltpu
from jax.sharding import PartitionSpec as P

HD = 64
EPS = 1e-06
CHUNK = 256
PAD = 8
BF = jnp.bfloat16
F32 = jnp.float32
MIB = 2**20
KEPT = 24
LANES = 128
SIN = (3.14158202, -5.16714279, 2.54189901, -0.55463616)
COS = (0.9999933, -4.93393802, 4.04128381, -1.22212701)


def nn(a, b):
    return lax.dot_general(a, b, (((1,), (0,)), ((), ())), preferred_element_type=F32)


def nt(a, b):
    return lax.dot_general(a, b, (((1,), (1,)), ((), ())), preferred_element_type=F32)


def tn(a, b):
    return lax.dot_general(a, b, (((0,), (0,)), ((), ())), preferred_element_type=F32)


def wave(turns, scale):
    big = F32(1.5 * 2.0**23)
    r = turns - ((turns + big) - big)
    u = r * r
    root = math.sqrt(2 * scale)
    a = [F32(v * root) for v in SIN]
    b = [F32(v * root) for v in COS]
    s = r * (a[0] + u * (a[1] + u * (a[2] + u * a[3])))
    c = b[0] + u * (b[1] + u * (b[2] + u * b[3]))
    return F32(scale) - s * s, s * c


def parts(f):
    hi = f.astype(BF)
    rest = f - hi.astype(F32)
    mid = rest.astype(BF)
    lo = (rest - mid.astype(F32)).astype(BF)
    return [hi, mid, lo]


def whole(shape):
    return pl.BlockSpec(shape, lambda *_: (0,) * len(shape))


def params(mib=60):
    return pltpu.CompilerParams(vmem_limit_bytes=mib * MIB)


def far(x):
    return pltpu.with_memory_space_constraint(x, pltpu.HBM)


def cost(flops, nbytes):
    return pl.CostEstimate(flops=int(flops), bytes_accessed=int(nbytes), transcendentals=0)


HERE = pl.BlockSpec(memory_space=pltpu.VMEM)
AWAY = pl.BlockSpec(memory_space=pl.ANY)
FAR = pl.BlockSpec(memory_space=pltpu.HBM)


def key_kernel(size, tok_hbm, wkt_hbm, wvt_hbm, freq_hbm, pick_hbm, *rest):
    tok_ref, kf_ref, vt_ref, sc_ref, tot_ref, own_ref, w_ref, freq_ref, pick_ref, sems = rest
    total = tok_ref.shape[0]
    wid = wkt_hbm.shape[0]
    heads = wid // HD
    half = freq_ref.shape[1]
    feat = 2 * half
    count = total // size
    weights = [
        pltpu.make_async_copy(w, w_ref.at[pl.ds(i * wid, wid)], sems.at[i])
        for i, w in enumerate((wkt_hbm, wvt_hbm))
    ]
    weights.append(pltpu.make_async_copy(freq_hbm, freq_ref, sems.at[2]))
    weights.append(pltpu.make_async_copy(pick_hbm, pick_ref, sems.at[3]))
    loads = [
        pltpu.make_async_copy(
            tok_hbm.at[pl.ds(i * size, size)], tok_ref.at[pl.ds(i * size, size)], sems.at[4 + i]
        )
        for i in range(count)
    ]
    for copy in [weights[0], loads[0], *weights[1:], *loads[1:]]:
        copy.start()
    for copy in weights:
        copy.wait()
    f3 = jnp.concatenate(parts(freq_ref[...] * F32(0.5 / math.pi)), axis=0)
    state = [jnp.zeros((HD, feat), F32) for _ in range(heads)]
    units = [(i, j, h) for i in range(count) for j in range(0, size, CHUNK) for h in range(heads)]
    per = len(units) // count
    key, val, phase, feats = {}, {}, {}, {}

    def project(i):
        loads[i].wait()
        span = slice(i * size, (i + 1) * size)
        out = nt(tok_ref[span, :], w_ref[...]).astype(BF)
        key[i] = out[:, :wid]
        val[i] = out[:, wid:].T
        vt_ref[:, span] = val[i]

    def turn(u):
        i, j, h = u
        k = key[i][j : j + CHUNK, h * HD : (h + 1) * HD]
        phase[u] = nn(jnp.concatenate([k] * 3, axis=1), f3)

    def feature(u):
        i, j, h = u
        c, s = wave(phase.pop(u), 1 / math.sqrt(half))
        feats[u] = jnp.concatenate([c.astype(BF), s.astype(BF)], axis=1)
        kf_ref[i * size + j : i * size + j + CHUNK, h * feat : (h + 1) * feat] = feats[u]

    def gather(u):
        i, j, h = u
        mine = slice(h * HD, (h + 1) * HD)
        sc_ref[(i * size + j) // CHUNK, mine, :] = state[h].astype(BF)
        state[h] = state[h] + nn(val[i][mine, j : j + CHUNK], feats.pop(u))

    project(0)
    for t in range(len(units) + 2):
        if t % per == per // 2 and t // per + 1 < count:
            project(t // per + 1)
        if t < len(units):
            turn(units[t])
        if 0 <= t - 1 < len(units):
            feature(units[t - 1])
        if 0 <= t - 2 < len(units):
            gather(units[t - 2])
    for h in range(heads):
        tot_ref[h * HD : (h + 1) * HD, :] = state[h].astype(BF)
    own_ref[...] = jnp.concatenate([pick_ref[c] for c in range(pick_ref.shape[0])], axis=1)


def key_pass(tokens, wkt, wvt, freq, picks, size):
    total, d = tokens.shape
    wid = wkt.shape[0]
    feat = 2 * freq.shape[1]
    heads = wid // HD
    return pl.pallas_call(
        functools.partial(key_kernel, size),
        in_specs=[FAR] * 5,
        out_specs=[HERE] * 6,
        out_shape=[
            jax.ShapeDtypeStruct(tokens.shape, BF),
            jax.ShapeDtypeStruct((total, heads * feat), BF),
            jax.ShapeDtypeStruct((wid, total), BF),
            jax.ShapeDtypeStruct((total // CHUNK, wid, feat), BF),
            jax.ShapeDtypeStruct((wid, feat), BF),
            jax.ShapeDtypeStruct((1, picks.size), jnp.int32),
        ],
        scratch_shapes=[
            pltpu.VMEM((2 * wid, d), BF),
            pltpu.VMEM(freq.shape, F32),
            pltpu.VMEM(picks.shape, jnp.int32),
            pltpu.SemaphoreType.DMA((4 + total // size,)),
        ],
        compiler_params=params(KEPT),
        cost_estimate=cost(5e9, 12e6),
        name="key_pass",
    )(*map(far, (tokens, wkt, wvt, freq, picks)))


def chosen(slot, pick_refs):
    row = pick_refs[0][...]
    for k in range(1, len(pick_refs)):
        row = jnp.where(slot == k, pick_refs[k][...], row)
    return row


def marks(row, rows):
    at = lax.broadcasted_iota(jnp.int32, (rows, row.shape[1]), 0)
    return (at == row).astype(F32).astype(BF)


def query_kernel(chunks, slots, picked, tok_ref, freq_ref, wqt_ref, kf_ref, vt_ref, sc_ref, *rest):
    pick_refs = rest[:picked]
    qft_ref, raw_ref = rest[-2 - (picked > 0) :][:2]
    wid = wqt_ref.shape[0]
    heads = wid // HD
    half = freq_ref.shape[1]
    feat = 2 * half
    rows = tok_ref.shape[0] // slots
    me = lax.axis_index("head")
    f3t = jnp.concatenate(parts(freq_ref[...].T * F32(0.5 / math.pi)), axis=1)
    place = [lax.broadcasted_iota(jnp.int32, (CHUNK, CHUNK), i) for i in (0, 1)]
    keep = place[0] <= place[1]
    units = [(c * CHUNK // rows, c * CHUNK % rows, h) for c in chunks for h in range(heads)]
    base = chunks[0] * CHUNK
    span = slice(base, base + len(chunks) * CHUNK)
    query = nt(tok_ref[span, :], wqt_ref[...]).astype(BF).T
    phase, feats, both = {}, {}, {}

    def spot(u):
        b, j, h = u
        return slice(h * HD, (h + 1) * HD), slice(b * rows + j, b * rows + j + CHUNK), slice(h * feat, (h + 1) * feat)

    def select(b):
        span = slice(b * rows, (b + 1) * rows)
        start = me * wid
        wide = -(-wid // LANES) * LANES
        low = pl.multiple_of(start // LANES * LANES, LANES)
        window = tok_ref[span, pl.ds(low, wide)]
        columns = window[:, :wid]
        for shift in range(math.gcd(wid, LANES), wide - wid + 1, math.gcd(wid, LANES)):
            columns = jnp.where(start % LANES == shift, window[:, shift : shift + wid], columns)
        line = chosen(me ^ b, pick_refs).T
        at = lax.broadcasted_iota(jnp.int32, (line.shape[0], rows), 1)
        rest[-1][b] = nn((at == line).astype(F32).astype(BF), columns).astype(BF).T

    def turn(u):
        mine, cols, _ = spot(u)
        q = query[mine, cols.start - base : cols.stop - base]
        phase[u] = nn(f3t, jnp.concatenate([q] * 3, axis=0))

    def feature(u):
        b, j, h = u
        c, s = wave(phase.pop(u), 1 / math.sqrt(half))
        feats[u] = jnp.concatenate([c.astype(BF), s.astype(BF)], axis=0)
        qft_ref[b, h * feat : (h + 1) * feat, j : j + CHUNK] = feats[u]

    def score(u):
        mine, cols, lines = spot(u)
        keys = jnp.concatenate([kf_ref[cols, lines], sc_ref[cols.start // CHUNK, mine, :]], axis=0)
        both[u] = nn(keys, feats.pop(u))

    def total(u):
        b, j, h = u
        mine, cols, _ = spot(u)
        got = both.pop(u)
        scores = jnp.where(keep, got[:CHUNK], 0.0).astype(BF)
        raw_ref[b, mine, j : j + CHUNK] = nn(vt_ref[mine, cols], scores) + got[CHUNK:]

    stages = (turn, feature, score, total)
    lag = 2
    for t in range(len(units) + lag * (len(stages) - 1)):
        if picked and t % heads == heads - 1 and t // heads < slots:
            select(t // heads)
        for i, stage in enumerate(stages):
            if 0 <= t - lag * i < len(units):
                stage(units[t - lag * i])


def query_pass(chunks, tokens, freq, wqt, kf, vt, sc, picks, slots, into):
    total, d = tokens.shape
    rows = total // slots
    wid = wqt.shape[0]
    feat = 2 * freq.shape[1]
    heads = wid // HD
    out_shape = [
        jax.ShapeDtypeStruct((slots, heads * feat, rows), BF),
        jax.ShapeDtypeStruct((slots, wid, rows), F32),
    ]
    if picks:
        out_shape.append(jax.ShapeDtypeStruct((slots, wid, picks[0].shape[1]), BF))
    args = [tokens, freq, wqt, kf, vt, sc, *picks, *into]
    return pl.pallas_call(
        functools.partial(query_kernel, chunks, slots, len(picks)),
        in_specs=[HERE] * (len(args) - len(into)) + [AWAY] * len(into),
        out_specs=[HERE] * len(out_shape),
        out_shape=out_shape,
        input_output_aliases={len(args) - len(into) + i: i for i in range(2) if into},
        compiler_params=params(KEPT),
        cost_estimate=cost(5e8 * len(chunks), 1e6 * len(chunks)),
        name="query_pass",
    )(*args)


def norm_kernel(slots, cap, rounds, raw_ref, qft_ref, seen_ref, *rest):
    got_refs, pick_refs = rest[:rounds], rest[rounds : rounds + slots]
    outs = rest[rounds + slots : rounds + slots + 3]
    sent, ready, acc, sems = rest[rounds + slots + 3 :]
    me, at = lax.axis_index("head"), lax.axis_index("seq")
    wid = raw_ref.shape[1]
    heads = wid // HD
    feat = got_refs[0].shape[1]
    before = jnp.zeros(got_refs[0].shape, F32)
    for i, got in enumerate(got_refs):
        before = before + jnp.where((at & (1 << i)) > 0, got[...].astype(F32), 0.0)
    before = before.astype(BF)
    goals = [outs[0], outs[1].at[pl.ds(0, wid)], outs[2], outs[1].at[pl.ds(wid, wid)]]
    copies = [pltpu.make_async_copy(ready.at[k], goals[k], sems.at[k]) for k in range(slots)]
    picked = {}

    def norm(k):
        block = me ^ k
        for h in range(heads):
            mine = slice(h * HD, (h + 1) * HD)
            raw = raw_ref[block, mine, :] + nn(before[mine, :], qft_ref[block, h * feat : (h + 1) * feat, :])
            meansq = jnp.mean(raw * raw, axis=0, keepdims=True)
            ready[k, mine, :] = (raw * lax.rsqrt(meansq + F32(EPS))).astype(BF)
        copies[k].start()

    def pick(k):
        picked[k] = nn(ready[k], marks(pick_refs[k][...], ready.shape[2])).astype(BF)

    def spread(k):
        both = jnp.concatenate([picked.pop(k), seen_ref[me ^ k]], axis=0)
        n = both.shape[1]
        experts = n // cap
        entry = lax.broadcasted_iota(jnp.int32, (1, n), 1)
        row = (entry % experts * slots + (me ^ k)) * cap + entry // experts
        part = nt(marks(row, acc.shape[0]), both)
        acc[...] = part if k == 0 else acc[...] + part

    stages = (norm, pick, spread)
    for t in range(slots + len(stages) - 1):
        for i, stage in enumerate(stages):
            if 0 <= t - i < slots:
                stage(t - i)
    sent[...] = acc[...].astype(BF)
    for copy in copies:
        copy.wait()


def norm_pass(raw, qft, seen, got, picks, cap):
    slots, wid, rows = raw.shape
    n = slots * picks[0].shape[1]
    return pl.pallas_call(
        functools.partial(norm_kernel, slots, cap, len(got)),
        in_specs=[HERE] * (3 + len(got) + slots),
        out_specs=[FAR] * 3 + [HERE],
        out_shape=[pltpu.HBM(x, BF) for x in ((wid, rows), (2 * wid, rows), (wid, rows))]
        + [jax.ShapeDtypeStruct((n, 2 * wid), BF)],
        scratch_shapes=[
            pltpu.VMEM((slots, wid, rows), BF),
            pltpu.VMEM((n, 2 * wid), F32),
            pltpu.SemaphoreType.DMA((slots + 1,)),
        ],
        compiler_params=params(KEPT + n * wid * 20 // MIB),
        cost_estimate=cost(3e9, 8e6),
        name="norm_pass",
    )(raw, qft, seen, *got, *picks)


def packing(d, cap):
    spare = PAD - cap
    columns = d // LANES
    tiles = -(-columns * cap // PAD)
    left = [(c, first) for c in range(tiles, columns) for first in range(0, cap, spare)]
    rest = [left[t : t + 1] for t in range(tiles)]
    return tiles, rest


def expert_kernel(cap, ups, downs, got_hbm, wo_hbm, wi_hbm, wd_hbm, out_ref, got, wo, wi, wd, taken, acc, sems):
    slots, ring, each, both = got.shape
    wid = both // 2
    n, d = ring * each, wo.shape[2]
    ff = wi.shape[1]
    landing = [pltpu.make_async_copy(got_hbm.at[:, h], got.at[h], sems.at[h]) for h in range(slots)]
    landing.append(pltpu.make_async_copy(wo_hbm, wo, sems.at[slots]))
    up = ff // ups
    rise = []
    for t in range(ups):
        cut = pl.ds(t * up, up)
        rise.append(pltpu.make_async_copy(wi_hbm.at[0, :, cut], wi.at[:, cut], sems.at[slots + 1 + t]))
    down = ff // downs
    fall = []
    for t in range(downs):
        cut = pl.ds(t * down, down)
        fall.append(pltpu.make_async_copy(wd_hbm.at[0, cut, :], wd.at[cut, :], sems.at[slots + 1 + ups + t]))
    for c in landing + rise + fall:
        c.start()
    for c in landing:
        c.wait()
    parts_in = [got[h].reshape(n, both) for h in range(slots)]
    mixed = jnp.concatenate([g.astype(F32)[:, wid:] for g in parts_in], axis=1)
    for h, g in enumerate(parts_in):
        mixed = mixed + nn(g[:, :wid], wo[h])
    taken[...] = mixed.astype(BF)
    inner = []
    for t in range(ups):
        rise[t].wait()
        part = nn(taken[...], wi[:, t * up : (t + 1) * up])
        inner.append(jax.nn.gelu(part, approximate=True).astype(BF))
    inner = jnp.concatenate(inner, axis=1)
    for t in range(downs):
        fall[t].wait()
        part = nn(inner[:, t * down : (t + 1) * down], wd[t * down : (t + 1) * down, :])
        acc[...] = part if t == 0 else acc[...] + part
    ready = acc[...].astype(BF)
    tiles, rest = packing(d, cap)
    blocks = n // cap
    line = lax.broadcasted_iota(jnp.int32, (blocks * PAD, n), 0)
    entry = lax.broadcasted_iota(jnp.int32, (blocks * PAD, n), 1)
    same = (line // PAD == entry // cap) & (line % PAD < cap)
    plain = (same & (line % PAD == entry % cap)).astype(F32).astype(BF)
    body = nn(plain, ready[:, : tiles * LANES])
    for t in range(tiles):
        tile = body[:, t * LANES : (t + 1) * LANES]
        for column, first in rest[t]:
            extra = (line // PAD == entry // cap) & (line % PAD >= cap) & (entry % cap == line % PAD - cap + first)
            tile = tile + nn(extra.astype(F32).astype(BF), ready[:, column * LANES : (column + 1) * LANES])
        out_ref[:, t * PAD : (t + 1) * PAD, :] = tile.reshape(blocks, PAD, LANES).astype(BF)


def expert_pass(arrived, w_out, w_in, w_down, cap, ups=3, downs=3):
    ring, slots, each, both = arrived.shape
    d, ff = w_in.shape[1:]
    blocks = ring * each // cap
    tiles = packing(d, cap)[0]
    return pl.pallas_call(
        functools.partial(expert_kernel, cap, ups, downs),
        in_specs=[AWAY] + [FAR] * 3,
        out_specs=HERE,
        out_shape=jax.ShapeDtypeStruct((blocks, tiles * PAD, LANES), BF),
        scratch_shapes=[
            pltpu.VMEM((slots, ring, each, both), BF),
            pltpu.VMEM(w_out.shape, BF),
            pltpu.VMEM((d, ff), BF),
            pltpu.VMEM((ff, d), BF),
            pltpu.VMEM((ring * each, d), BF),
            pltpu.VMEM((ring * each, d), F32),
            pltpu.SemaphoreType.DMA((slots + 1 + ups + downs,)),
        ],
        compiler_params=params(40),
        cost_estimate=cost(2e9, 12e6),
        name="expert_pass",
    )(arrived, *map(far, (w_out, w_in, w_down)))


def hidden_kernel(tok_hbm, wo_hbm, own_hbm, near_hbm, far_hbm, router_ref, pick_ref, *rest):
    hid_ref, comb_ref, tok, wo, attn, sems = rest
    me = lax.axis_index("head")
    rows = tok.shape[0]
    group, wid = wo_hbm.shape[:2]
    first = pl.multiple_of(me * rows, rows)
    pieces = [own_hbm, near_hbm.at[pl.ds(0, wid)], far_hbm.at[pl.ds(0, wid)], far_hbm.at[pl.ds(wid, wid)]]
    copies = [pltpu.make_async_copy(tok_hbm.at[pl.ds(first, rows)], tok, sems.at[0])]
    for k in range(group):
        line = pl.ds(k * wid, wid)
        copies.append(pltpu.make_async_copy(wo_hbm.at[me ^ k], wo.at[line], sems.at[1 + k]))
        copies.append(pltpu.make_async_copy(pieces[k], attn.at[line], sems.at[1 + group + k]))
    for copy in copies:
        copy.start()
    for copy in copies:
        copy.wait()
    experts, n = router_ref.shape[0], pick_ref.shape[1]
    spreads = marks(lax.broadcasted_iota(jnp.int32, (1, n), 1) // PAD, experts)
    hidden = (tok[...].astype(F32) + tn(attn[...], wo[...])).astype(BF)
    hid_ref[...] = hidden
    gate = jax.nn.sigmoid(nt(hidden, router_ref[...])).astype(BF)
    at = lax.broadcasted_iota(jnp.int32, (rows, n), 0)
    weight = nn(gate, spreads)
    for i in range(comb_ref.shape[0]):
        comb_ref[i] = jnp.where(pick_ref[i : i + 1, :] == at, weight, 0.0).astype(BF)


def hidden_pass(tokens, w_out, own, near, across, router_t, pick_row):
    d = tokens.shape[1]
    group, wid = w_out.shape[:2]
    rows = tokens.shape[0] // group
    kinds, n = pick_row.shape
    return pl.pallas_call(
        hidden_kernel,
        in_specs=[FAR] * 2 + [AWAY] * 3 + [HERE] * 2,
        out_specs=[HERE] * 2,
        out_shape=[jax.ShapeDtypeStruct((rows, d), BF), jax.ShapeDtypeStruct((kinds, rows, n), BF)],
        scratch_shapes=[
            pltpu.VMEM((rows, d), BF),
            pltpu.VMEM((group * wid, d), BF),
            pltpu.VMEM((group * wid, rows), BF),
            pltpu.SemaphoreType.DMA((1 + 2 * group,)),
        ],
        compiler_params=params(),
        cost_estimate=cost(2e9, 6e6),
        name="hidden_pass",
    )(far(tokens), far(w_out), own, near, across, router_t, pick_row)


def combine_kernel(tiles, cap, hid_hbm, comb_hbm, back_hbm, out_hbm, hid, comb, back, out, in_sems, out_sems):
    rows = hid.shape[0]
    tile = rows // tiles
    cuts = [pl.ds(t * tile, tile) for t in range(tiles)]
    need = pltpu.make_async_copy(back_hbm, back, in_sems.at[0])
    loads = [
        [
            pltpu.make_async_copy(comb_hbm.at[:, c], comb.at[:, c], in_sems.at[1 + 2 * t]),
            pltpu.make_async_copy(hid_hbm.at[c], hid.at[c], in_sems.at[2 + 2 * t]),
        ]
        for t, c in enumerate(cuts)
    ]
    stores = [pltpu.make_async_copy(out.at[c], out_hbm.at[c], out_sems.at[t]) for t, c in enumerate(cuts)]
    need.start()
    for pair in loads:
        for copy in pair:
            copy.start()
    packs, rest = packing(hid.shape[1], cap)
    left = {}
    for j, held in enumerate(rest):
        for column, first in held:
            left.setdefault(column, []).append((j, first))
    need.wait()
    got = [back[:, j * PAD : (j + 1) * PAD, :].reshape(comb.shape[2], LANES) for j in range(packs)]
    for t, cut in enumerate(cuts):
        for copy in loads[t]:
            copy.wait()
        for j in range(packs):
            lanes = slice(j * LANES, (j + 1) * LANES)
            out[cut, lanes] = (hid[cut, lanes].astype(F32) + nn(comb[0, cut, :], got[j])).astype(BF)
        for column, places in left.items():
            lanes = slice(column * LANES, (column + 1) * LANES)
            moe = sum(nn(comb[1 + first // (PAD - cap), cut, :], got[j]) for j, first in places)
            out[cut, lanes] = (hid[cut, lanes].astype(F32) + moe).astype(BF)
        stores[t].start()
    for store in stores:
        store.wait()


def combine_pass(hidden, comb, back, cap, tiles=3):
    rows, d = hidden.shape
    return pl.pallas_call(
        functools.partial(combine_kernel, tiles, cap),
        in_specs=[FAR, FAR, AWAY],
        out_specs=AWAY,
        out_shape=jax.ShapeDtypeStruct((rows, d), BF),
        scratch_shapes=[
            pltpu.VMEM(hidden.shape, BF),
            pltpu.VMEM(comb.shape, BF),
            pltpu.VMEM(back.shape, BF),
            pltpu.VMEM(hidden.shape, BF),
            pltpu.SemaphoreType.DMA((1 + 2 * tiles,)),
            pltpu.SemaphoreType.DMA((tiles,)),
        ],
        compiler_params=params(40),
        cost_estimate=cost(1e9, 4e6),
        name="combine_pass",
    )(far(hidden), far(comb), back)


def per_device(tokens, w_query, w_key, w_value, freq, w_out, router, w_in, w_down, picks):
    total, d = tokens.shape
    group = lax.axis_size("head")
    ring = lax.axis_size("seq")
    rows = total // group
    experts, _, cap = picks.shape
    wid = w_query.shape[1]

    spare = PAD - cap
    own_picks = picks[:, 0, :]
    kinds = [jnp.pad(own_picks, ((0, 0), (0, spare)), constant_values=-1)]
    for first in range(0, cap, spare):
        kinds.append(jnp.pad(own_picks[:, first : first + spare], ((0, 0), (cap, 0)), constant_values=-1))
    pick_row = jnp.stack(kinds).reshape(len(kinds), experts * PAD)
    swap = lambda x, k: lax.ppermute(x, "head", [(i, i ^ k) for i in range(group)])

    tok_here, kf, vt, sc, held, own = key_pass(
        tokens, w_key.T, w_value.T, freq, picks.transpose(2, 1, 0), math.gcd(total, 4 * CHUNK)
    )
    near = [own] + [swap(own, k) for k in range(1, group)]
    got, made = [], []
    chunks = total // CHUNK
    rounds = ring.bit_length() - 1
    for i in range(rounds):
        got.append(lax.ppermute(held, "seq", [(j, j ^ (1 << i)) for j in range(ring)]))
        part = range(chunks * i // rounds, chunks * (i + 1) // rounds)
        made = query_pass(
            part, tok_here, freq, w_query.T, kf, vt, sc, near if i == rounds - 1 else [], group, made
        )
        both = held.astype(F32) + got[-1].astype(F32)
        held, *made = lax.optimization_barrier([both.astype(BF), *made])
    qft, raw, seen = made
    mine, near_out, across, sent = norm_pass(raw, qft, seen, got, near, cap)

    sent = sent.reshape(experts, group * cap, 2 * wid)
    arrived = lax.all_to_all(sent, ("seq", "head"), split_axis=0, concat_axis=0, tiled=True)
    near_got = swap(near_out, 1)
    across = swap(jnp.concatenate([across, near_got[wid:]]), 2)
    arrived, pick_row = lax.optimization_barrier((arrived, pick_row))
    w_out = w_out.reshape(group, wid, d)
    result = expert_pass(
        arrived.reshape(ring, group, group * cap, 2 * wid), w_out, w_in, w_down, cap
    )
    back = lax.all_to_all(result, ("seq", "head"), split_axis=0, concat_axis=0, tiled=True)
    hidden, comb = hidden_pass(tokens, w_out, mine, near_got, across, router.T, pick_row)
    return combine_pass(hidden, comb, back, cap)


def solution(mesh):
    in_specs = (
        P("seq", None),
        P(None, "head"),
        P(None, "head"),
        P(None, "head"),
        P(),
        P(),
        P(),
        P(("seq", "head"), None, None),
        P(("seq", "head"), None, None),
        P(None, ("seq", "head"), None),
    )
    out_specs = P(("seq", "head"), None)
    return jax.shard_map(
        per_device, mesh=mesh, in_specs=in_specs, out_specs=out_specs, check_vma=False
    )
```

```python
import functools
import math

import jax
import jax.numpy as jnp
from jax import lax
from jax.experimental import pallas as pl
from jax.experimental.pallas import tpu as pltpu
from jax.sharding import PartitionSpec as P

HD = 64
EPS = 1e-06
CHUNK = 256
PAD = 8
BF = jnp.bfloat16
F32 = jnp.float32
MIB = 2**20
KEPT = 24
LANES = 128
SIN = (3.14158202, -5.16714279, 2.54189901, -0.55463616)
COS = (0.9999933, -4.93393802, 4.04128381, -1.22212701)


def nn(a, b):
    return lax.dot_general(a, b, (((1,), (0,)), ((), ())), preferred_element_type=F32)


def nt(a, b):
    return lax.dot_general(a, b, (((1,), (1,)), ((), ())), preferred_element_type=F32)


def tn(a, b):
    return lax.dot_general(a, b, (((0,), (0,)), ((), ())), preferred_element_type=F32)


def wave(turns, scale):
    big = F32(1.5 * 2.0**23)
    r = turns - ((turns + big) - big)
    u = r * r
    root = math.sqrt(2 * scale)
    a = [F32(v * root) for v in SIN]
    b = [F32(v * root) for v in COS]
    s = r * (a[0] + u * (a[1] + u * (a[2] + u * a[3])))
    c = b[0] + u * (b[1] + u * (b[2] + u * b[3]))
    return F32(scale) - s * s, s * c


def parts(f):
    hi = f.astype(BF)
    rest = f - hi.astype(F32)
    mid = rest.astype(BF)
    lo = (rest - mid.astype(F32)).astype(BF)
    return [hi, mid, lo]


def whole(shape):
    return pl.BlockSpec(shape, lambda *_: (0,) * len(shape))


def params(mib=60):
    return pltpu.CompilerParams(vmem_limit_bytes=mib * MIB)


def far(x):
    return pltpu.with_memory_space_constraint(x, pltpu.HBM)


def cost(flops, nbytes):
    return pl.CostEstimate(flops=int(flops), bytes_accessed=int(nbytes), transcendentals=0)


HERE = pl.BlockSpec(memory_space=pltpu.VMEM)
AWAY = pl.BlockSpec(memory_space=pl.ANY)
FAR = pl.BlockSpec(memory_space=pltpu.HBM)


def key_kernel(size, tok_hbm, wkt_hbm, wvt_hbm, freq_hbm, pick_hbm, *rest):
    tok_ref, kf_ref, vt_ref, sc_ref, tot_ref, own_ref, w_ref, freq_ref, pick_ref, sems = rest
    total = tok_ref.shape[0]
    wid = wkt_hbm.shape[0]
    heads = wid // HD
    half = freq_ref.shape[1]
    feat = 2 * half
    count = total // size
    weights = [
        pltpu.make_async_copy(w, w_ref.at[pl.ds(i * wid, wid)], sems.at[i])
        for i, w in enumerate((wkt_hbm, wvt_hbm))
    ]
    weights.append(pltpu.make_async_copy(freq_hbm, freq_ref, sems.at[2]))
    weights.append(pltpu.make_async_copy(pick_hbm, pick_ref, sems.at[3]))
    loads = [
        pltpu.make_async_copy(
            tok_hbm.at[pl.ds(i * size, size)], tok_ref.at[pl.ds(i * size, size)], sems.at[4 + i]
        )
        for i in range(count)
    ]
    for copy in [weights[0], loads[0], *weights[1:], *loads[1:]]:
        copy.start()
    for copy in weights:
        copy.wait()
    f3 = jnp.concatenate(parts(freq_ref[...] * F32(0.5 / math.pi)), axis=0)
    state = [jnp.zeros((HD, feat), F32) for _ in range(heads)]
    units = [(i, j, h) for i in range(count) for j in range(0, size, CHUNK) for h in range(heads)]
    per = len(units) // count
    key, val, phase, feats = {}, {}, {}, {}

    def project(i):
        loads[i].wait()
        span = slice(i * size, (i + 1) * size)
        out = nt(tok_ref[span, :], w_ref[...]).astype(BF)
        key[i] = out[:, :wid]
        val[i] = out[:, wid:].T
        vt_ref[:, span] = val[i]

    def turn(u):
        i, j, h = u
        k = key[i][j : j + CHUNK, h * HD : (h + 1) * HD]
        phase[u] = nn(jnp.concatenate([k] * 3, axis=1), f3)

    def feature(u):
        i, j, h = u
        c, s = wave(phase.pop(u), 1 / math.sqrt(half))
        feats[u] = jnp.concatenate([c.astype(BF), s.astype(BF)], axis=1)
        kf_ref[i * size + j : i * size + j + CHUNK, h * feat : (h + 1) * feat] = feats[u]

    def gather(u):
        i, j, h = u
        mine = slice(h * HD, (h + 1) * HD)
        sc_ref[(i * size + j) // CHUNK, mine, :] = state[h].astype(BF)
        state[h] = state[h] + nn(val[i][mine, j : j + CHUNK], feats.pop(u))

    project(0)
    for t in range(len(units) + 2):
        if t % per == per // 2 and t // per + 1 < count:
            project(t // per + 1)
        if t < len(units):
            turn(units[t])
        if 0 <= t - 1 < len(units):
            feature(units[t - 1])
        if 0 <= t - 2 < len(units):
            gather(units[t - 2])
    for h in range(heads):
        tot_ref[h * HD : (h + 1) * HD, :] = state[h].astype(BF)
    own_ref[...] = jnp.concatenate([pick_ref[c] for c in range(pick_ref.shape[0])], axis=1)


def key_pass(tokens, wkt, wvt, freq, picks, size):
    total, d = tokens.shape
    wid = wkt.shape[0]
    feat = 2 * freq.shape[1]
    heads = wid // HD
    return pl.pallas_call(
        functools.partial(key_kernel, size),
        in_specs=[FAR] * 5,
        out_specs=[HERE] * 6,
        out_shape=[
            jax.ShapeDtypeStruct(tokens.shape, BF),
            jax.ShapeDtypeStruct((total, heads * feat), BF),
            jax.ShapeDtypeStruct((wid, total), BF),
            jax.ShapeDtypeStruct((total // CHUNK, wid, feat), BF),
            jax.ShapeDtypeStruct((wid, feat), BF),
            jax.ShapeDtypeStruct((1, picks.size), jnp.int32),
        ],
        scratch_shapes=[
            pltpu.VMEM((2 * wid, d), BF),
            pltpu.VMEM(freq.shape, F32),
            pltpu.VMEM(picks.shape, jnp.int32),
            pltpu.SemaphoreType.DMA((4 + total // size,)),
        ],
        compiler_params=params(KEPT),
        cost_estimate=cost(5e9, 12e6),
        name="key_pass",
    )(*map(far, (tokens, wkt, wvt, freq, picks)))


def chosen(slot, pick_refs):
    row = pick_refs[0][...]
    for k in range(1, len(pick_refs)):
        row = jnp.where(slot == k, pick_refs[k][...], row)
    return row


def marks(row, rows):
    at = lax.broadcasted_iota(jnp.int32, (rows, row.shape[1]), 0)
    return (at == row).astype(F32).astype(BF)


def query_kernel(chunks, slots, picked, tok_ref, freq_ref, wqt_ref, kf_ref, vt_ref, sc_ref, *rest):
    pick_refs = rest[:picked]
    qft_ref, raw_ref = rest[-2 - (picked > 0) :][:2]
    wid = wqt_ref.shape[0]
    heads = wid // HD
    half = freq_ref.shape[1]
    feat = 2 * half
    rows = tok_ref.shape[0] // slots
    me = lax.axis_index("head")
    f3t = jnp.concatenate(parts(freq_ref[...].T * F32(0.5 / math.pi)), axis=1)
    place = [lax.broadcasted_iota(jnp.int32, (CHUNK, CHUNK), i) for i in (0, 1)]
    keep = place[0] <= place[1]
    units = [(c * CHUNK // rows, c * CHUNK % rows, h) for c in chunks for h in range(heads)]
    base = chunks[0] * CHUNK
    span = slice(base, base + len(chunks) * CHUNK)
    query = nt(tok_ref[span, :], wqt_ref[...]).astype(BF).T
    phase, feats, both = {}, {}, {}

    def spot(u):
        b, j, h = u
        return slice(h * HD, (h + 1) * HD), slice(b * rows + j, b * rows + j + CHUNK), slice(h * feat, (h + 1) * feat)

    def select(b):
        span = slice(b * rows, (b + 1) * rows)
        start = me * wid
        wide = -(-wid // LANES) * LANES
        low = pl.multiple_of(start // LANES * LANES, LANES)
        window = tok_ref[span, pl.ds(low, wide)]
        columns = window[:, :wid]
        for shift in range(math.gcd(wid, LANES), wide - wid + 1, math.gcd(wid, LANES)):
            columns = jnp.where(start % LANES == shift, window[:, shift : shift + wid], columns)
        line = chosen(me ^ b, pick_refs).T
        at = lax.broadcasted_iota(jnp.int32, (line.shape[0], rows), 1)
        rest[-1][b] = nn((at == line).astype(F32).astype(BF), columns).astype(BF).T

    def turn(u):
        mine, cols, _ = spot(u)
        q = query[mine, cols.start - base : cols.stop - base]
        phase[u] = nn(f3t, jnp.concatenate([q] * 3, axis=0))

    def feature(u):
        b, j, h = u
        c, s = wave(phase.pop(u), 1 / math.sqrt(half))
        feats[u] = jnp.concatenate([c.astype(BF), s.astype(BF)], axis=0)
        qft_ref[b, h * feat : (h + 1) * feat, j : j + CHUNK] = feats[u]

    def score(u):
        mine, cols, lines = spot(u)
        keys = jnp.concatenate([kf_ref[cols, lines], sc_ref[cols.start // CHUNK, mine, :]], axis=0)
        both[u] = nn(keys, feats.pop(u))

    def total(u):
        b, j, h = u
        mine, cols, _ = spot(u)
        got = both.pop(u)
        scores = jnp.where(keep, got[:CHUNK], 0.0).astype(BF)
        raw_ref[b, mine, j : j + CHUNK] = nn(vt_ref[mine, cols], scores) + got[CHUNK:]

    stages = (turn, feature, score, total)
    lag = 2
    for t in range(len(units) + lag * (len(stages) - 1)):
        if picked and t % heads == heads - 1 and t // heads < slots:
            select(t // heads)
        for i, stage in enumerate(stages):
            if 0 <= t - lag * i < len(units):
                stage(units[t - lag * i])


def query_pass(chunks, tokens, freq, wqt, kf, vt, sc, picks, slots, into):
    total, d = tokens.shape
    rows = total // slots
    wid = wqt.shape[0]
    feat = 2 * freq.shape[1]
    heads = wid // HD
    out_shape = [
        jax.ShapeDtypeStruct((slots, heads * feat, rows), BF),
        jax.ShapeDtypeStruct((slots, wid, rows), F32),
    ]
    if picks:
        out_shape.append(jax.ShapeDtypeStruct((slots, wid, picks[0].shape[1]), BF))
    args = [tokens, freq, wqt, kf, vt, sc, *picks, *into]
    return pl.pallas_call(
        functools.partial(query_kernel, chunks, slots, len(picks)),
        in_specs=[HERE] * (len(args) - len(into)) + [AWAY] * len(into),
        out_specs=[HERE] * len(out_shape),
        out_shape=out_shape,
        input_output_aliases={len(args) - len(into) + i: i for i in range(2) if into},
        compiler_params=params(KEPT),
        cost_estimate=cost(5e8 * len(chunks), 1e6 * len(chunks)),
        name="query_pass",
    )(*args)


def norm_kernel(slots, cap, rounds, raw_ref, qft_ref, seen_ref, *rest):
    got_refs, pick_refs = rest[:rounds], rest[rounds : rounds + slots]
    outs = rest[rounds + slots : rounds + slots + 3]
    sent, ready, acc, sems = rest[rounds + slots + 3 :]
    me, at = lax.axis_index("head"), lax.axis_index("seq")
    wid = raw_ref.shape[1]
    heads = wid // HD
    feat = got_refs[0].shape[1]
    before = jnp.zeros(got_refs[0].shape, F32)
    for i, got in enumerate(got_refs):
        before = before + jnp.where((at & (1 << i)) > 0, got[...].astype(F32), 0.0)
    before = before.astype(BF)
    goals = [outs[0], outs[1].at[pl.ds(0, wid)], outs[2], outs[1].at[pl.ds(wid, wid)]]
    copies = [pltpu.make_async_copy(ready.at[k], goals[k], sems.at[k]) for k in range(slots)]
    picked = {}

    def norm(k):
        block = me ^ k
        for h in range(heads):
            mine = slice(h * HD, (h + 1) * HD)
            raw = raw_ref[block, mine, :] + nn(before[mine, :], qft_ref[block, h * feat : (h + 1) * feat, :])
            meansq = jnp.mean(raw * raw, axis=0, keepdims=True)
            ready[k, mine, :] = (raw * lax.rsqrt(meansq + F32(EPS))).astype(BF)
        copies[k].start()

    def pick(k):
        picked[k] = nn(ready[k], marks(pick_refs[k][...], ready.shape[2])).astype(BF)

    def spread(k):
        both = jnp.concatenate([picked.pop(k), seen_ref[me ^ k]], axis=0)
        n = both.shape[1]
        experts = n // cap
        entry = lax.broadcasted_iota(jnp.int32, (1, n), 1)
        row = (entry % experts * slots + (me ^ k)) * cap + entry // experts
        part = nt(marks(row, acc.shape[0]), both)
        acc[...] = part if k == 0 else acc[...] + part

    stages = (norm, pick, spread)
    for t in range(slots + len(stages) - 1):
        for i, stage in enumerate(stages):
            if 0 <= t - i < slots:
                stage(t - i)
    sent[...] = acc[...].astype(BF)
    for copy in copies:
        copy.wait()


def norm_pass(raw, qft, seen, got, picks, cap):
    slots, wid, rows = raw.shape
    n = slots * picks[0].shape[1]
    return pl.pallas_call(
        functools.partial(norm_kernel, slots, cap, len(got)),
        in_specs=[HERE] * (3 + len(got) + slots),
        out_specs=[FAR] * 3 + [HERE],
        out_shape=[pltpu.HBM(x, BF) for x in ((wid, rows), (2 * wid, rows), (wid, rows))]
        + [jax.ShapeDtypeStruct((n, 2 * wid), BF)],
        scratch_shapes=[
            pltpu.VMEM((slots, wid, rows), BF),
            pltpu.VMEM((n, 2 * wid), F32),
            pltpu.SemaphoreType.DMA((slots + 1,)),
        ],
        compiler_params=params(KEPT + n * wid * 20 // MIB),
        cost_estimate=cost(3e9, 8e6),
        name="norm_pass",
    )(raw, qft, seen, *got, *picks)


def packing(d, cap):
    spare = PAD - cap
    columns = d // LANES
    tiles = -(-columns * cap // PAD)
    left = [(c, first) for c in range(tiles, columns) for first in range(0, cap, spare)]
    rest = [left[t : t + 1] for t in range(tiles)]
    return tiles, rest


def expert_kernel(cap, ups, downs, got_hbm, wo_hbm, wi_hbm, wd_hbm, out_ref, got, wo, wi, wd, taken, acc, sems):
    slots, ring, each, both = got.shape
    wid = both // 2
    n, d = ring * each, wo.shape[2]
    ff = wi.shape[1]
    landing = [pltpu.make_async_copy(got_hbm.at[:, h], got.at[h], sems.at[h]) for h in range(slots)]
    landing.append(pltpu.make_async_copy(wo_hbm, wo, sems.at[slots]))
    up = ff // ups
    rise = []
    for t in range(ups):
        cut = pl.ds(t * up, up)
        rise.append(pltpu.make_async_copy(wi_hbm.at[0, :, cut], wi.at[:, cut], sems.at[slots + 1 + t]))
    down = ff // downs
    fall = []
    for t in range(downs):
        cut = pl.ds(t * down, down)
        fall.append(pltpu.make_async_copy(wd_hbm.at[0, cut, :], wd.at[cut, :], sems.at[slots + 1 + ups + t]))
    for c in landing + rise + fall:
        c.start()
    for c in landing:
        c.wait()
    parts_in = [got[h].reshape(n, both) for h in range(slots)]
    mixed = jnp.concatenate([g.astype(F32)[:, wid:] for g in parts_in], axis=1)
    for h, g in enumerate(parts_in):
        mixed = mixed + nn(g[:, :wid], wo[h])
    taken[...] = mixed.astype(BF)
    inner = []
    for t in range(ups):
        rise[t].wait()
        part = nn(taken[...], wi[:, t * up : (t + 1) * up])
        inner.append(jax.nn.gelu(part, approximate=True).astype(BF))
    inner = jnp.concatenate(inner, axis=1)
    for t in range(downs):
        fall[t].wait()
        part = nn(inner[:, t * down : (t + 1) * down], wd[t * down : (t + 1) * down, :])
        acc[...] = part if t == 0 else acc[...] + part
    ready = acc[...].astype(BF)
    tiles, rest = packing(d, cap)
    blocks = n // cap
    line = lax.broadcasted_iota(jnp.int32, (blocks * PAD, n), 0)
    entry = lax.broadcasted_iota(jnp.int32, (blocks * PAD, n), 1)
    same = (line // PAD == entry // cap) & (line % PAD < cap)
    plain = (same & (line % PAD == entry % cap)).astype(F32).astype(BF)
    body = nn(plain, ready[:, : tiles * LANES])
    for t in range(tiles):
        tile = body[:, t * LANES : (t + 1) * LANES]
        for column, first in rest[t]:
            extra = (line // PAD == entry // cap) & (line % PAD >= cap) & (entry % cap == line % PAD - cap + first)
            tile = tile + nn(extra.astype(F32).astype(BF), ready[:, column * LANES : (column + 1) * LANES])
        out_ref[:, t * PAD : (t + 1) * PAD, :] = tile.reshape(blocks, PAD, LANES).astype(BF)


def expert_pass(arrived, w_out, w_in, w_down, cap, ups=3, downs=3):
    ring, slots, each, both = arrived.shape
    d, ff = w_in.shape[1:]
    blocks = ring * each // cap
    tiles = packing(d, cap)[0]
    return pl.pallas_call(
        functools.partial(expert_kernel, cap, ups, downs),
        in_specs=[AWAY] + [FAR] * 3,
        out_specs=HERE,
        out_shape=jax.ShapeDtypeStruct((blocks, tiles * PAD, LANES), BF),
        scratch_shapes=[
            pltpu.VMEM((slots, ring, each, both), BF),
            pltpu.VMEM(w_out.shape, BF),
            pltpu.VMEM((d, ff), BF),
            pltpu.VMEM((ff, d), BF),
            pltpu.VMEM((ring * each, d), BF),
            pltpu.VMEM((ring * each, d), F32),
            pltpu.SemaphoreType.DMA((slots + 1 + ups + downs,)),
        ],
        compiler_params=params(40),
        cost_estimate=cost(2e9, 12e6),
        name="expert_pass",
    )(arrived, *map(far, (w_out, w_in, w_down)))


def hidden_kernel(tok_hbm, wo_hbm, own_hbm, near_hbm, far_hbm, router_ref, pick_ref, *rest):
    hid_ref, comb_ref, tok, wo, attn, sems = rest
    me = lax.axis_index("head")
    rows = tok.shape[0]
    group, wid = wo_hbm.shape[:2]
    first = pl.multiple_of(me * rows, rows)
    pieces = [own_hbm, near_hbm.at[pl.ds(0, wid)], far_hbm.at[pl.ds(0, wid)], far_hbm.at[pl.ds(wid, wid)]]
    copies = [pltpu.make_async_copy(tok_hbm.at[pl.ds(first, rows)], tok, sems.at[0])]
    for k in range(group):
        line = pl.ds(k * wid, wid)
        copies.append(pltpu.make_async_copy(wo_hbm.at[me ^ k], wo.at[line], sems.at[1 + k]))
        copies.append(pltpu.make_async_copy(pieces[k], attn.at[line], sems.at[1 + group + k]))
    for copy in copies:
        copy.start()
    for copy in copies:
        copy.wait()
    experts, n = router_ref.shape[0], pick_ref.shape[1]
    spreads = marks(lax.broadcasted_iota(jnp.int32, (1, n), 1) // PAD, experts)
    hidden = (tok[...].astype(F32) + tn(attn[...], wo[...])).astype(BF)
    hid_ref[...] = hidden
    gate = jax.nn.sigmoid(nt(hidden, router_ref[...])).astype(BF)
    at = lax.broadcasted_iota(jnp.int32, (rows, n), 0)
    weight = nn(gate, spreads)
    for i in range(comb_ref.shape[0]):
        comb_ref[i] = jnp.where(pick_ref[i : i + 1, :] == at, weight, 0.0).astype(BF)


def hidden_pass(tokens, w_out, own, near, across, router_t, pick_row):
    d = tokens.shape[1]
    group, wid = w_out.shape[:2]
    rows = tokens.shape[0] // group
    kinds, n = pick_row.shape
    return pl.pallas_call(
        hidden_kernel,
        in_specs=[FAR] * 2 + [AWAY] * 3 + [HERE] * 2,
        out_specs=[HERE] * 2,
        out_shape=[jax.ShapeDtypeStruct((rows, d), BF), jax.ShapeDtypeStruct((kinds, rows, n), BF)],
        scratch_shapes=[
            pltpu.VMEM((rows, d), BF),
            pltpu.VMEM((group * wid, d), BF),
            pltpu.VMEM((group * wid, rows), BF),
            pltpu.SemaphoreType.DMA((1 + 2 * group,)),
        ],
        compiler_params=params(),
        cost_estimate=cost(2e9, 6e6),
        name="hidden_pass",
    )(far(tokens), far(w_out), own, near, across, router_t, pick_row)


def combine_kernel(tiles, cap, hid_hbm, comb_hbm, back_hbm, out_hbm, hid, comb, back, out, in_sems, out_sems):
    rows = hid.shape[0]
    tile = rows // tiles
    cuts = [pl.ds(t * tile, tile) for t in range(tiles)]
    need = pltpu.make_async_copy(back_hbm, back, in_sems.at[0])
    loads = [
        [
            pltpu.make_async_copy(comb_hbm.at[:, c], comb.at[:, c], in_sems.at[1 + 2 * t]),
            pltpu.make_async_copy(hid_hbm.at[c], hid.at[c], in_sems.at[2 + 2 * t]),
        ]
        for t, c in enumerate(cuts)
    ]
    stores = [pltpu.make_async_copy(out.at[c], out_hbm.at[c], out_sems.at[t]) for t, c in enumerate(cuts)]
    need.start()
    for pair in loads:
        for copy in pair:
            copy.start()
    packs, rest = packing(hid.shape[1], cap)
    left = {}
    for j, held in enumerate(rest):
        for column, first in held:
            left.setdefault(column, []).append((j, first))
    need.wait()
    got = [back[:, j * PAD : (j + 1) * PAD, :].reshape(comb.shape[2], LANES) for j in range(packs)]
    for t, cut in enumerate(cuts):
        for copy in loads[t]:
            copy.wait()
        for j in range(packs):
            lanes = slice(j * LANES, (j + 1) * LANES)
            out[cut, lanes] = (hid[cut, lanes].astype(F32) + nn(comb[0, cut, :], got[j])).astype(BF)
        for column, places in left.items():
            lanes = slice(column * LANES, (column + 1) * LANES)
            moe = sum(nn(comb[1 + first // (PAD - cap), cut, :], got[j]) for j, first in places)
            out[cut, lanes] = (hid[cut, lanes].astype(F32) + moe).astype(BF)
        stores[t].start()
    for store in stores:
        store.wait()


def combine_pass(hidden, comb, back, cap, tiles=3):
    rows, d = hidden.shape
    return pl.pallas_call(
        functools.partial(combine_kernel, tiles, cap),
        in_specs=[FAR, FAR, AWAY],
        out_specs=AWAY,
        out_shape=jax.ShapeDtypeStruct((rows, d), BF),
        scratch_shapes=[
            pltpu.VMEM(hidden.shape, BF),
            pltpu.VMEM(comb.shape, BF),
            pltpu.VMEM(back.shape, BF),
            pltpu.VMEM(hidden.shape, BF),
            pltpu.SemaphoreType.DMA((1 + 2 * tiles,)),
            pltpu.SemaphoreType.DMA((tiles,)),
        ],
        compiler_params=params(40),
        cost_estimate=cost(1e9, 4e6),
        name="combine_pass",
    )(far(hidden), far(comb), back)


def per_device(tokens, w_query, w_key, w_value, freq, w_out, router, w_in, w_down, picks):
    total, d = tokens.shape
    group = lax.axis_size("head")
    ring = lax.axis_size("seq")
    rows = total // group
    experts, _, cap = picks.shape
    wid = w_query.shape[1]

    spare = PAD - cap
    own_picks = picks[:, 0, :]
    kinds = [jnp.pad(own_picks, ((0, 0), (0, spare)), constant_values=-1)]
    for first in range(0, cap, spare):
        kinds.append(jnp.pad(own_picks[:, first : first + spare], ((0, 0), (cap, 0)), constant_values=-1))
    pick_row = jnp.stack(kinds).reshape(len(kinds), experts * PAD)
    swap = lambda x, k: lax.ppermute(x, "head", [(i, i ^ k) for i in range(group)])

    tok_here, kf, vt, sc, held, own = key_pass(
        tokens, w_key.T, w_value.T, freq, picks.transpose(2, 1, 0), math.gcd(total, 4 * CHUNK)
    )
    near = [own] + [swap(own, k) for k in range(1, group)]
    got, made = [], []
    chunks = total // CHUNK
    rounds = ring.bit_length() - 1
    edges = [chunks * i // rounds - (0 < i < rounds) for i in range(rounds + 1)]
    for i in range(rounds):
        got.append(lax.ppermute(held, "seq", [(j, j ^ (1 << i)) for j in range(ring)]))
        part = range(edges[i], edges[i + 1])
        made = query_pass(
            part, tok_here, freq, w_query.T, kf, vt, sc, near if i == rounds - 1 else [], group, made
        )
        both = held.astype(F32) + got[-1].astype(F32)
        held, *made = lax.optimization_barrier([both.astype(BF), *made])
    qft, raw, seen = made
    mine, near_out, across, sent = norm_pass(raw, qft, seen, got, near, cap)

    sent = sent.reshape(experts, group * cap, 2 * wid)
    arrived = lax.all_to_all(sent, ("seq", "head"), split_axis=0, concat_axis=0, tiled=True)
    near_got = swap(near_out, 1)
    across = swap(jnp.concatenate([across, near_got[wid:]]), 2)
    arrived, pick_row = lax.optimization_barrier((arrived, pick_row))
    w_out = w_out.reshape(group, wid, d)
    result = expert_pass(
        arrived.reshape(ring, group, group * cap, 2 * wid), w_out, w_in, w_down, cap
    )
    back = lax.all_to_all(result, ("seq", "head"), split_axis=0, concat_axis=0, tiled=True)
    hidden, comb = hidden_pass(tokens, w_out, mine, near_got, across, router.T, pick_row)
    return combine_pass(hidden, comb, back, cap)


def solution(mesh):
    in_specs = (
        P("seq", None),
        P(None, "head"),
        P(None, "head"),
        P(None, "head"),
        P(),
        P(),
        P(),
        P(("seq", "head"), None, None),
        P(("seq", "head"), None, None),
        P(None, ("seq", "head"), None),
    )
    out_specs = P(("seq", "head"), None)
    return jax.shard_map(
        per_device, mesh=mesh, in_specs=in_specs, out_specs=out_specs, check_vma=False
    )
```
